32 devices in a mesh: dp: 8 (over z, x), fsdp: 4 (over y, core).
Axes of the slice: x: 2, y: 2, z: 4, core: 2. Of those that a mesh axis runs over, the one named last changes fastest.
Arguments:
- ar_params: float32 [12587008], P(('dp', 'fsdp'))
- nar_params: float32 [12611584], P(('dp', 'fsdp'))
- ar_moments: float32 [2, 12587008], P(None, ('dp', 'fsdp')), as said below
- nar_moments: float32 [2, 12611584], P(None, ('dp', 'fsdp')), as said below
- hidden_in: bfloat16 [32, 384, 1024], P(('dp', 'fsdp')), may hold values from -6 to 6
- out_grad: bfloat16 [32, 384, 1024], P(('dp', 'fsdp')), may hold values from -6 to 6
- phon_len: int32 [32], P(('dp', 'fsdp')), may hold values from 5 to 109, as said below
- acou_len: int32 [32], P(('dp', 'fsdp')), may hold values from 83 to 379, as said below
- frame_mask: int32 [32, 384], P(('dp', 'fsdp')), may hold values 0 or 1
- section: int32 [32], P(('dp', 'fsdp')), may hold values from 0 to 6
Outputs:
- hidden_out: bfloat16 [32, 384, 1024], P(('dp', 'fsdp'))
- in_grad: float32 [32, 384, 1024], P(('dp', 'fsdp'))
- ar_grad: float32 [12587008], P(('dp', 'fsdp'))
- nar_grad: float32 [12611584], P(('dp', 'fsdp'))
- ar_step: float32 [12587008], P(('dp', 'fsdp'))
- nar_step: float32 [12611584], P(('dp', 'fsdp'))
- ar_new_moments: float32 [2, 12587008], P(None, ('dp', 'fsdp'))
- nar_new_moments: float32 [2, 12611584], P(None, ('dp', 'fsdp'))
- nar_table_grad: float32 [4, 7, 1024], replicated
The draws below stay inside these ranges and needn't reach their ends.
Inputs may be any that keep to these rules, and one draw needn't show every extreme that they name: `phon_len`: in every draw some block has 5 phonemes and another 109. phon_len + acou_len lies between 192 and 384; in every draw one block is full and another holds 192 positions. `ar_moments`: the second row holds positive values. `nar_moments`: the second row holds positive values.
All inputs are finite; a program needn't handle non-finite values. No bound on the sum of `frame_mask` on one device may be relied on, other than what follows from the above.
Results may differ from the reference program's by a relative error of at most 0.024.
The reference program's roundings to bfloat16 on the way count: a program that leaves them out, or rounds other values in their place, can miss the bound.
Values may be sent and summed in bfloat16 or wider, within the bound.
A program may use at most 320 MiB of HBM per device.

```python
import math
import jax
import jax.numpy as jnp
from jax import lax

D = 1024
FF = 4096
HEADS = 16
SECTIONS = 7
HEAD_DIM = 64
FRAMES = 384
STEP = 100
ITEMS = 32
PH_LO = 5
PH_HI = 109
ARP = 12587008
NARP = 12611584


def block_lengths(key):
    subkeys = jax.random.split(key, 3)
    phonemes = jax.random.randint(subkeys[0], (ITEMS,), PH_LO, PH_HI + 1)
    totals = jax.random.randint(subkeys[1], (ITEMS,), FRAMES // 2, FRAMES + 1)
    shuffled = jax.random.permutation(subkeys[2], ITEMS)
    phonemes = phonemes.at[shuffled[0]].set(PH_LO).at[shuffled[1]].set(PH_HI)
    totals = totals.at[shuffled[0]].set(FRAMES).at[shuffled[1]].set(FRAMES // 2)
    return (phonemes.astype(jnp.int32), totals.astype(jnp.int32))


def draw_phon_len(key, part):
    phonemes, totals = block_lengths(key)
    return phonemes


def draw_acou_len(key, part):
    phonemes, totals = block_lengths(key)
    return (totals - phonemes).astype(jnp.int32)


def param_values(raw_noise, matrices, table_rows):
    position = jnp.arange(raw_noise.shape[0])
    cut_one = 3 * D * D
    cut_two = 4 * D * D
    cut_three = cut_two + D * FF
    factor = jnp.where(position < cut_one, 1.4 / math.sqrt(D), 1.5 / math.sqrt(FF))
    factor = jnp.where((position >= cut_one) & (position < cut_two), 4.0 / math.sqrt(D), factor)
    factor = jnp.where((position >= cut_two) & (position < cut_three), 1.0 / math.sqrt(D), factor)
    table_row = jnp.maximum(position - matrices, 0) // (table_rows * D)
    in_table = position >= matrices
    norm_part = jnp.where(table_row % 2 == 0, 1.0 + 0.15 * raw_noise, 0.3 * raw_noise)
    return jnp.where(in_table, norm_part, factor * raw_noise).astype(jnp.float32)


def draw_ar_params(key, part):
    key = jax.random.fold_in(key, 11)
    raw_noise = jax.random.normal(key, (ARP,), jnp.float32)
    return param_values(raw_noise, 4 * D * D + 2 * D * FF, 1)


def draw_nar_params(key, part):
    key = jax.random.fold_in(key, 12)
    raw_noise = jax.random.normal(key, (NARP,), jnp.float32)
    return param_values(raw_noise, 4 * D * D + 2 * D * FF, SECTIONS)


def moment_values(key, entries):
    subkeys = jax.random.split(key, 2)
    spread = 0.05 * math.sqrt(ITEMS * FRAMES)
    first = spread * jax.random.normal(subkeys[0], (entries,), jnp.float32)
    second = jnp.square(spread * jnp.exp(jax.random.uniform(subkeys[1], (entries,), jnp.float32, -1.0, 1.0)))
    return jnp.stack([first, second]).astype(jnp.float32)


def draw_ar_moments(key, part):
    key = jax.random.fold_in(key, 21)
    return moment_values(key, ARP)


def draw_nar_moments(key, part):
    key = jax.random.fold_in(key, 22)
    return moment_values(key, NARP)


def place_ends(values, rng, smallest, top_value):
    place = [jax.random.randint(jax.random.fold_in(rng, axis), (), 0, length) for axis, length in enumerate(values.shape)]
    main_axis = values.shape.index(max(values.shape))
    neighbour = place[:main_axis] + [(place[main_axis] + 1) % values.shape[main_axis]] + place[main_axis + 1:]
    return values.at[tuple(place)].set(smallest).at[tuple(neighbour)].set(top_value)


def block_scale(stream_key, shape, shards, low, largest):
    def one(axis_at, shards_of):
        heights = jax.random.uniform(jax.random.fold_in(jax.random.fold_in(stream_key, 6), axis_at), (shards_of,), jnp.float32, low / len(shards), largest / len(shards))
        return jnp.repeat(jnp.exp(heights), shape[axis_at] // shards_of).reshape((-1,) + (1,) * (len(shape) - axis_at - 1))

    gain = one(*shards[0])
    for cut in shards[1:]:
        gain = gain * one(*cut)
    return gain


def scatter_about(key, shape, deviation, reach, cuts=(), held_as=jnp.bfloat16):
    array = jax.random.normal(key, shape, jnp.float32) * deviation
    if len(cuts) > 0:
        array = block_scale(key, shape, cuts, -0.22, 0.18) * array
    return jnp.clip(array, min=-reach, max=reach).astype(held_as)


def setup_inputs(seed: int = 0) -> dict:
    arg_keys = jax.random.split(jax.random.key(seed), 11)
    return {
        "ar_params": draw_ar_params(jax.random.fold_in(arg_keys[10], 71), 0),
        "nar_params": draw_nar_params(jax.random.fold_in(arg_keys[10], 71), 0),
        "ar_moments": draw_ar_moments(jax.random.fold_in(arg_keys[10], 71), 0),
        "nar_moments": draw_nar_moments(jax.random.fold_in(arg_keys[10], 71), 0),
        "hidden_in": scatter_about(arg_keys[4], (ITEMS, FRAMES, D), 1.0, 6.0, ((0, 32),)),
        "out_grad": scatter_about(arg_keys[5], (ITEMS, FRAMES, D), 1.0, 6.0, ((0, 32),)),
        "phon_len": draw_phon_len(jax.random.fold_in(arg_keys[10], 71), 0),
        "acou_len": draw_acou_len(jax.random.fold_in(arg_keys[10], 71), 0),
        "frame_mask": place_ends((jax.random.randint(arg_keys[8], (ITEMS, FRAMES), 0, 8) < 7).astype(jnp.int32), jax.random.fold_in(arg_keys[8], 1), 0, 1),
        "section": place_ends(jax.random.randint(arg_keys[9], (ITEMS,), 0, SECTIONS), jax.random.fold_in(arg_keys[9], 1), 0, SECTIONS - 1).astype(jnp.int32),
    }


norm_eps = 1e-05
beta_one = 0.9
beta_two = 0.999
adam_eps = 1e-08

@jax.custom_vjp
def low(v):
    return lax.optimization_barrier(v.astype(jnp.bfloat16)).astype(jnp.float32)

@jax.custom_vjp
def low_back(v):
    return v

def low_keep(v):
    return (low(v), None)

def low_pass(kept, grad):
    return (grad,)

def back_keep(v):
    return (v, None)

def back_low(kept, grad):
    return (low(grad),)
low.defvjp(low_keep, low_pass)
low_back.defvjp(back_keep, back_low)

def matmul_high(left, right):
    return jnp.dot(left, right, precision=lax.Precision.HIGHEST, preferred_element_type=jnp.float32)

def normalize(layer_in, gain_rows, bias_rows):
    row_mean = lax.optimization_barrier(jnp.mean(layer_in, axis=-1, keepdims=True))
    centred = layer_in - row_mean
    row_var = lax.optimization_barrier(jnp.mean(centred * centred, axis=-1, keepdims=True))
    return centred * lax.rsqrt(row_var + norm_eps) * gain_rows[:, None, :] + bias_rows[:, None, :]

def unpack(flat_params, table_rows):
    cut_one = 3 * D * D
    cut_two = 4 * D * D
    cut_three = cut_two + D * FF
    cut_four = cut_three + FF * D
    cut_five = cut_four + 4 * table_rows * D
    matrices = (flat_params[:cut_one].reshape(D, 3 * D), flat_params[cut_one:cut_two].reshape(D, D), flat_params[cut_two:cut_three].reshape(D, FF), flat_params[cut_three:cut_four].reshape(FF, D))
    return (matrices, flat_params[cut_four:cut_five].reshape(4, table_rows, D))

def layer_pass(layer_in, matrices, norm_gains, allowed):
    w_qkv, w_out, w_up, w_down = matrices
    items_here = layer_in.shape[0]
    row_count = items_here * FRAMES
    normed_one = low(normalize(layer_in, norm_gains[0], norm_gains[1])).reshape(row_count, D)
    qkv_all = low_back(low(matmul_high(normed_one, w_qkv))).reshape(items_here, FRAMES, 3, HEADS, HEAD_DIM)
    queries = qkv_all[:, :, 0]
    key_rows = qkv_all[:, :, 1]
    values = qkv_all[:, :, 2]
    scores = jnp.einsum('bqhd,bkhd->bhqk', queries, key_rows, precision=lax.Precision.HIGHEST)
    scores = low_back(scores * HEAD_DIM ** (-0.5))
    scores = jnp.where(allowed[:, None], scores, -jnp.inf)
    row_top = lax.optimization_barrier(jnp.max(scores, axis=-1, keepdims=True))
    exponent = jnp.exp(scores - row_top)
    attn_probs = exponent / lax.optimization_barrier(jnp.sum(exponent, axis=-1, keepdims=True))
    attended = jnp.einsum('bhqk,bkhd->bqhd', low(attn_probs), values, precision=lax.Precision.HIGHEST)
    attended = low_back(low(attended)).reshape(row_count, D)
    middle = layer_in + low_back(matmul_high(attended, w_out)).reshape(items_here, FRAMES, D)
    normed_two = low(normalize(middle, norm_gains[2], norm_gains[3])).reshape(row_count, D)
    upper = low_back(matmul_high(normed_two, w_up))
    activated = low(jax.nn.gelu(upper))
    return middle + low_back(matmul_high(activated, w_down)).reshape(items_here, FRAMES, D)

def forward(ar_flat, nar_flat, hidden_start, phonemes, acoustic, masks, sections):
    items_here = hidden_start.shape[0]
    position = jnp.arange(FRAMES)
    key_live = (position[None, :] < (phonemes + acoustic)[:, None]) & ((masks == 1) | (position[None, :] == 0))
    causal = position[None, :] <= position[:, None]
    prefix = position[None, None, :] < phonemes[:, None, None]
    ar_allowed = key_live[:, None, :] & (causal[None] | prefix)
    nar_allowed = jnp.broadcast_to(key_live[:, None, :], (items_here, FRAMES, FRAMES))
    ar_matrices, ar_table = unpack(low(ar_flat), 1)
    nar_matrices, nar_table = unpack(low(nar_flat), SECTIONS)
    ar_gains = jnp.broadcast_to(ar_table[:, 0, None, :], (4, items_here, D))
    onehot = (sections[:, None] == jnp.arange(SECTIONS)[None, :]).astype(jnp.float32)
    nar_gains = jnp.einsum('bs,rsd->rbd', onehot, nar_table, precision=lax.Precision.HIGHEST)
    first_out = layer_pass(hidden_start, ar_matrices, ar_gains, ar_allowed)
    return layer_pass(first_out, nar_matrices, nar_gains, nar_allowed)

def adam_update(moments, gradient):
    first = beta_one * moments[0] + (1.0 - beta_one) * gradient
    second = beta_two * moments[1] + (1.0 - beta_two) * gradient * gradient
    first_hat = first / (1.0 - beta_one ** STEP)
    second_hat = second / (1.0 - beta_two ** STEP)
    direction = first_hat / (jnp.sqrt(second_hat) + adam_eps)
    return (direction, jnp.stack([first, second]))

def reference(ar_params, nar_params, ar_moments, nar_moments, hidden_in, out_grad, phon_len, acou_len, frame_mask, section):
    per_group = 1
    for candidate in range(1, ITEMS + 1):
        if ITEMS % candidate == 0 and candidate * FRAMES <= 2048:
            per_group = candidate
    groups = ITEMS // per_group

    def regroup(array_in):
        return array_in.reshape((groups, per_group) + array_in.shape[1:])

    def group_step(running, pieces):
        ar_sum, nar_sum = running
        inputs, grads_given, phonemes, acoustic, masks, sections = pieces

        def apply_layers(ar_flat, nar_flat, hidden_start):
            return forward(ar_flat, nar_flat, hidden_start, phonemes, acoustic, masks, sections)
        result, pullback = jax.vjp(apply_layers, ar_params, nar_params, inputs.astype(jnp.float32))
        ar_part, nar_part, input_part = pullback(grads_given.astype(jnp.float32))
        return ((ar_sum + ar_part, nar_sum + nar_part), (result.astype(jnp.bfloat16), input_part))
    start_sums = (jnp.zeros_like(ar_params), jnp.zeros_like(nar_params))
    (ar_grad, nar_grad), (outputs, in_grads) = lax.scan(group_step, start_sums, (regroup(hidden_in), regroup(out_grad), regroup(phon_len), regroup(acou_len), regroup(frame_mask), regroup(section)))
    hidden_out = outputs.reshape(ITEMS, FRAMES, D)
    in_grad = in_grads.reshape(ITEMS, FRAMES, D)
    table_start = 4 * D * D + 2 * D * FF
    nar_table_grad = nar_grad[table_start:table_start + 4 * SECTIONS * D].reshape(4, SECTIONS, D)
    ar_step, ar_new_moments = adam_update(ar_moments, ar_grad)
    nar_step, nar_new_moments = adam_update(nar_moments, nar_grad)
    return (hidden_out, in_grad, ar_grad, nar_grad, ar_step, nar_step, ar_new_moments, nar_new_moments, nar_table_grad)
```

```python
import functools

import jax
import jax.numpy as jnp
from jax import lax
from jax.experimental import pallas as pl
from jax.experimental.pallas import tpu as pltpu
from jax.sharding import PartitionSpec as P

D = 1024
FF = 4096
HEADS = 16
SECTIONS = 7
HEAD_DIM = 64
FRAMES = 384
STEP = 100


norm_eps = 1e-05
beta_one = 0.9
beta_two = 0.999
adam_eps = 1e-08


def normalize(layer_in, gain_rows, bias_rows):
    row_mean = jnp.mean(layer_in, axis=-1, keepdims=True)
    centred = layer_in - row_mean
    row_var = jnp.mean(centred * centred, axis=-1, keepdims=True)
    return centred * lax.rsqrt(row_var + norm_eps) * gain_rows[:, None, :] + bias_rows[:, None, :]


def unpack(flat_params, table_rows):
    cut_one = 3 * D * D
    cut_two = 4 * D * D
    cut_three = cut_two + D * FF
    cut_four = cut_three + FF * D
    cut_five = cut_four + 4 * table_rows * D
    matrices = (
        flat_params[:cut_one].reshape(D, 3 * D),
        flat_params[cut_one:cut_two].reshape(D, D),
        flat_params[cut_two:cut_three].reshape(D, FF),
        flat_params[cut_three:cut_four].reshape(FF, D),
    )
    return (matrices, flat_params[cut_four:cut_five].reshape(4, table_rows, D))


def collect(shard):
    tiles = shard.reshape(-1, 128)
    whole = lax.all_gather(tiles, ("dp", "fsdp"), axis=0, tiled=True)
    return whole.reshape(-1)


def spread(gradient, owned):
    total = owned * lax.axis_size("dp") * lax.axis_size("fsdp")
    padded = jnp.pad(gradient, (0, total - gradient.shape[0])).reshape(-1, 128)
    mine = lax.psum_scatter(padded, ("dp", "fsdp"), scatter_dimension=0, tiled=True)
    return mine.reshape(-1)


def trunk(layer_in, matrices, norm_gains, allowed, saved_total):
    w_qkv, w_out, w_up, w_down = matrices
    items_here = layer_in.shape[0]
    row_count = items_here * FRAMES
    score_scale = HEAD_DIM ** (-0.5)
    normed_one, first_back = jax.vjp(normalize, layer_in, norm_gains[0], norm_gains[1])
    normed_low = normed_one.astype(jnp.bfloat16).reshape(row_count, D)
    qkv_low = jnp.dot(normed_low, w_qkv, preferred_element_type=jnp.float32).astype(jnp.bfloat16)
    qkv_split = qkv_low.reshape(items_here, FRAMES, 3, HEADS, HEAD_DIM)
    queries = qkv_split[:, :, 0]
    key_rows = qkv_split[:, :, 1]
    values = qkv_split[:, :, 2]
    scores = (
        jnp.einsum("bqhd,bkhd->bhqk", queries, key_rows, preferred_element_type=jnp.float32)
        * score_scale
    )
    scores = jnp.where(allowed[:, None], scores, -jnp.inf)
    if saved_total is None:
        row_top = jnp.max(scores, axis=-1, keepdims=True)
        saved_total = row_top + jnp.log(jnp.sum(jnp.exp(scores - row_top), axis=-1, keepdims=True))
    attn_probs = jnp.exp(scores - saved_total)
    probs_low = attn_probs.astype(jnp.bfloat16)
    attended = jnp.einsum("bhqk,bkhd->bqhd", probs_low, values, preferred_element_type=jnp.float32)
    attended = attended.astype(jnp.bfloat16).reshape(row_count, D)
    middle = layer_in + jnp.dot(attended, w_out, preferred_element_type=jnp.float32).reshape(
        items_here, FRAMES, D
    )
    normed_two, second_back = jax.vjp(normalize, middle, norm_gains[2], norm_gains[3])
    second_low = normed_two.astype(jnp.bfloat16).reshape(row_count, D)
    upper = jnp.dot(second_low, w_up, preferred_element_type=jnp.float32)
    activated, gelu_back = jax.vjp(jax.nn.gelu, upper)
    act_low = activated.astype(jnp.bfloat16)
    layer_out = middle + jnp.dot(act_low, w_down, preferred_element_type=jnp.float32).reshape(
        items_here, FRAMES, D
    )
    stored = (
        first_back,
        normed_low,
        queries,
        key_rows,
        values,
        attn_probs,
        probs_low,
        attended,
        second_back,
        second_low,
        gelu_back,
        act_low,
    )
    return (layer_out, saved_total, stored)


def layer_back(stored, matrices, grad_out):
    w_qkv, w_out, w_up, w_down = matrices
    (
        first_back,
        normed_low,
        queries,
        key_rows,
        values,
        attn_probs,
        probs_low,
        attended,
        second_back,
        second_low,
        gelu_back,
        act_low,
    ) = stored
    items_here = grad_out.shape[0]
    row_count = items_here * FRAMES
    score_scale = HEAD_DIM ** (-0.5)
    grad_low = grad_out.reshape(row_count, D).astype(jnp.bfloat16)
    grad_down = jnp.einsum("rf,rd->fd", act_low, grad_low, preferred_element_type=jnp.float32)
    grad_act = jnp.einsum("rd,fd->rf", grad_low, w_down, preferred_element_type=jnp.float32)
    grad_upper = gelu_back(grad_act)[0].astype(jnp.bfloat16)
    grad_up = jnp.einsum("rd,rf->df", second_low, grad_upper, preferred_element_type=jnp.float32)
    grad_second = jnp.einsum("rf,df->rd", grad_upper, w_up, preferred_element_type=jnp.float32)
    norm_part, grad_gain_two, grad_bias_two = second_back(
        grad_second.reshape(items_here, FRAMES, D)
    )
    grad_middle = grad_out + norm_part
    branch_low = grad_middle.reshape(row_count, D).astype(jnp.bfloat16)
    grad_wout = jnp.einsum("rc,rd->cd", attended, branch_low, preferred_element_type=jnp.float32)
    grad_attended = jnp.einsum("rd,cd->rc", branch_low, w_out, preferred_element_type=jnp.float32)
    grad_attended = grad_attended.astype(jnp.bfloat16).reshape(items_here, FRAMES, HEADS, HEAD_DIM)
    grad_values = jnp.einsum(
        "bhqk,bqhd->bkhd", probs_low, grad_attended, preferred_element_type=jnp.float32
    )
    grad_probs = jnp.einsum(
        "bqhd,bkhd->bhqk", grad_attended, values, preferred_element_type=jnp.float32
    )
    row_inner = jnp.sum(attn_probs * grad_probs, axis=-1, keepdims=True)
    grad_scores = (attn_probs * (grad_probs - row_inner)).astype(jnp.bfloat16)
    grad_queries = (
        jnp.einsum("bhqk,bkhd->bqhd", grad_scores, key_rows, preferred_element_type=jnp.float32)
        * score_scale
    )
    grad_keys = (
        jnp.einsum("bhqk,bqhd->bkhd", grad_scores, queries, preferred_element_type=jnp.float32)
        * score_scale
    )
    grad_qkv = (
        jnp.stack([grad_queries, grad_keys, grad_values], axis=2)
        .astype(jnp.bfloat16)
        .reshape(row_count, 3 * D)
    )
    grad_wqkv = jnp.einsum("rc,rd->cd", normed_low, grad_qkv, preferred_element_type=jnp.float32)
    grad_first = jnp.einsum("rd,cd->rc", grad_qkv, w_qkv, preferred_element_type=jnp.float32)
    norm_in, grad_gain_one, grad_bias_one = first_back(grad_first.reshape(items_here, FRAMES, D))
    grad_in = grad_middle + norm_in
    grad_mats = (grad_wqkv, grad_wout, grad_up, grad_down)
    grad_gains = jnp.stack([grad_gain_one, grad_bias_one, grad_gain_two, grad_bias_two])
    return (grad_in, grad_mats, grad_gains)


def adam_update(moments, gradient):
    first = beta_one * moments[0] + (1.0 - beta_one) * gradient
    second = beta_two * moments[1] + (1.0 - beta_two) * gradient * gradient
    first_hat = first / (1.0 - beta_one**STEP)
    second_hat = second / (1.0 - beta_two**STEP)
    direction = first_hat / (jnp.sqrt(second_hat) + adam_eps)
    return (direction, jnp.stack([first, second]))


def per_device(
    ar_params,
    nar_params,
    ar_moments,
    nar_moments,
    hidden_in,
    out_grad,
    phon_len,
    acou_len,
    frame_mask,
    section,
):
    items_here = hidden_in.shape[0]
    position = jnp.arange(FRAMES)
    key_live = (position[None, :] < (phon_len + acou_len)[:, None]) & (
        (frame_mask == 1) | (position[None, :] == 0)
    )
    causal = position[None, :] <= position[:, None]
    prefix = position[None, None, :] < phon_len[:, None, None]
    ar_allowed = key_live[:, None, :] & (causal[None] | prefix)
    nar_allowed = jnp.broadcast_to(key_live[:, None, :], (items_here, FRAMES, FRAMES))
    ar_matrices, ar_table = unpack(collect(ar_params.astype(jnp.bfloat16)), 1)
    ar_gains = ar_table[:, 0, None, :].astype(jnp.float32)
    nar_matrices, nar_table = unpack(collect(nar_params.astype(jnp.bfloat16)), SECTIONS)
    onehot = (section[:, None] == jnp.arange(SECTIONS)[None, :]).astype(jnp.float32)
    nar_gains = jnp.einsum(
        "bs,rsd->rbd", onehot, nar_table.astype(jnp.float32), precision=lax.Precision.HIGHEST
    )
    first_in = hidden_in.astype(jnp.float32)
    first_out, unused, ar_stored = trunk(first_in, ar_matrices, ar_gains, ar_allowed, None)
    final, unused, nar_stored = trunk(first_out, nar_matrices, nar_gains, nar_allowed, None)
    hidden_out = final.astype(jnp.bfloat16)
    grad_mid, nar_grad_mats, nar_grad_gains = layer_back(nar_stored, nar_matrices, out_grad.astype(jnp.float32))
    nar_grad_table = jnp.einsum(
        "bs,rbd->rsd", onehot, nar_grad_gains, precision=lax.Precision.HIGHEST
    )
    nar_table_grad = lax.psum(nar_grad_table, ("dp", "fsdp"))
    nar_grad = spread(
        jnp.concatenate([m.reshape(-1) for m in nar_grad_mats] + [nar_grad_table.reshape(-1)]), nar_params.shape[0]
    )
    in_grad, ar_grad_mats, ar_grad_gains = layer_back(ar_stored, ar_matrices, grad_mid)
    ar_grad = spread(
        jnp.concatenate([m.reshape(-1) for m in ar_grad_mats] + [jnp.sum(ar_grad_gains, axis=1).reshape(-1)]),
        ar_params.shape[0],
    )
    ar_step, ar_new_moments = adam_update(ar_moments, ar_grad)
    nar_step, nar_new_moments = adam_update(nar_moments, nar_grad)
    return (
        hidden_out,
        in_grad,
        ar_grad,
        nar_grad,
        ar_step,
        nar_step,
        ar_new_moments,
        nar_new_moments,
        nar_table_grad,
    )


MESH = pl.DeviceIdType.MESH
NZ = 4

class Place:
    def __init__(self):
        dp = lax.axis_index("dp"); fs = lax.axis_index("fsdp")
        self.z, self.x = dp // 2, dp % 2
        self.y, self.c = fs // 2, fs % 2
        z, x, y, c = self.z, self.x, self.y, self.c
        self.a = (z * 2 + x + (1 - c) * (1 - 2 * x), (y + c * (1 - 2 * y)) * 2 + c)
        self.b = (z * 2 + x + c * (1 - 2 * x), (y + (1 - c) * (1 - 2 * y)) * 2 + c)
        self.up = (dp + 2, fs)
        self.down = (dp - 2, fs)
        self.core = (dp, y * 2 + 1 - c)
    def chip(self, zp, da, db):
        c = self.c
        dx = da * (1 - c) + db * c
        dy = db * (1 - c) + da * c
        xp = self.x + dx * (1 - 2 * self.x)
        yp = self.y + dy * (1 - 2 * self.y)
        return (zp * 2 + xp) * 2 + yp

def byz(zp, z):
    return (zp == 1) | (zp == 2) | ((zp == 0) & (z == 1)) | ((zp == 3) & (z == 2))

def barrier(me):
    bar = pltpu.get_barrier_semaphore()
    def sig(dev): pl.semaphore_signal(bar, inc=1, device_id=dev, device_id_type=MESH)
    sig(me.a); sig(me.b); sig(me.core)
    pl.when(me.z < NZ - 1)(lambda: sig(me.up))
    pl.when(me.z > 0)(lambda: sig(me.down))
    pl.semaphore_wait(bar, 4 + (me.z + 1) // 2 % 2)

ORDER = [(0,0,0),(0,1,0),(0,0,1),(1,0,0),(0,1,1),(1,1,0),(1,0,1),(2,0,0),(1,1,1),(2,1,0),(2,0,1),(3,0,0),(2,1,1),(3,1,0),(3,0,1),(3,1,1)]

def events(me):
    out = []
    for d, da, db in ORDER:
        for sg in ((1,) if d == 0 else (1, -1)):
            zp = me.z + sg * d
            valid = None if d == 0 else ((zp < NZ) if sg > 0 else (zp >= 0))
            out.append((d, sg, da, db, zp, valid))
    return out

def children(me, d, sg, da, db, zp):
    z = me.z
    kids = []
    up_ok = (d == 0) or sg < 0
    dn_ok = (d == 0) or sg > 0
    if (da, db) == (0, 0):
        if up_ok: kids.append(("up", me.up, z < NZ - 1))
        if dn_ok: kids.append(("down", me.down, z > 0))
        kids.append(("b", me.b, None))
        kids.append(("a", me.a, None))
    elif (da, db) == (1, 0):
        kids.append(("b", me.b, None if d == 0 else jnp.logical_not(byz(zp, z))))
    elif (da, db) == (1, 1):
        if up_ok: kids.append(("up", me.up, (z < NZ - 1) & byz(zp, z + 1)))
        if dn_ok: kids.append(("down", me.down, (z > 0) & byz(zp, z - 1)))
    return kids

LINKS = {"a": 0, "b": 1, "up": 2, "down": 3, "core": 4}

def when(cond, f):
    def g(): f()
    if cond is None: g()
    else: pl.when(cond)(g)

def ag_kernel(nl, U, sub, *refs):
    srcs, outs = refs[:nl], refs[nl:2*nl]
    ssem, rsem, csem, lsem = refs[2*nl:]
    me = Place()
    barrier(me)
    step = U // sub
    evs = events(me)
    def copy(l, h, src, s, dev, link, o, sem):
        return pltpu.make_async_remote_copy(src_ref=src, dst_ref=outs[l].at[pl.ds(s * U + h * step, step)],
            send_sem=ssem.at[l, h, o, LINKS[link]], recv_sem=sem.at[l, h, o], device_id=dev, device_id_type=MESH)
    def handle(l, h, ev, phase):
        d, sg, da, db, zp, valid = ev
        own = (d, da, db) == (0, 0, 0)
        o = me.chip(zp, da, db)
        s = o * 2 + me.c
        def go():
            if own: src = srcs[l].at[pl.ds(h * step, step)]
            else: src = outs[l].at[pl.ds(s * U + h * step, step)]
            if phase == 0 and not own:
                copy(l, h, src, s, me.core, "core", o, rsem).wait_recv()
            for link, dev, cond in children(me, d, sg, da, db, zp) + [("core", me.core, None)]:
                cp = copy(l, h, src, s, dev, link, o, csem if link == "core" else rsem)
                when(cond, cp.start if phase == 0 else cp.wait_send)
        when(valid, go)
    locs = []
    for l in range(nl):
        s = me.chip(me.z, 0, 0) * 2 + me.c
        cp = pltpu.make_async_copy(srcs[l], outs[l].at[pl.ds(s * U, U)], lsem.at[l]); cp.start(); locs.append(cp)
    seq = []
    for l in range(nl):
        for ei, ev in enumerate(evs):
            for h in range(sub): seq.append((l, h, ev))
    for l, h, ev in seq: handle(l, h, ev, 0)
    for l, h, ev in seq: handle(l, h, ev, 1)
    for l in range(nl):
        for o in range(16):
            for h in range(sub):
                s = o * 2 + 1 - me.c
                copy(l, h, outs[l].at[pl.ds(s * U + h*step, step)], s, me.core, "core", o, csem).wait_recv()
    for cp in locs: cp.wait()

def all_gather(shards, U, sub=1, cid=1):
    nl = len(shards)
    return pl.pallas_call(functools.partial(ag_kernel, nl, U, sub),
        out_shape=[jax.ShapeDtypeStruct((U * 32, D), jnp.bfloat16)] * nl,
        in_specs=[pl.BlockSpec(memory_space=pl.ANY)] * nl, out_specs=[pl.BlockSpec(memory_space=pl.ANY)] * nl,
        scratch_shapes=[pltpu.SemaphoreType.DMA((nl, sub, 16, 5)), pltpu.SemaphoreType.DMA((nl, sub, 16)), pltpu.SemaphoreType.DMA((nl, sub, 16)), pltpu.SemaphoreType.DMA((nl,))],
        compiler_params=pltpu.CompilerParams(collective_id=cid, has_side_effects=True), name="gather_weights")(*shards)

def rs_kernel(U, sub, part, out, P, Dn, R, ssem, rsem, csem, cssem, lsem):
    me = Place()
    barrier(me)
    step = U // sub
    evs = events(me)[::-1]
    def load(o):
        return pltpu.make_async_copy(part.at[pl.ds((o * 2 + me.c) * U, U)], P.at[o], lsem.at[o])
    def dcopy(o):
        return pltpu.make_async_remote_copy(src_ref=part.at[pl.ds((o * 2 + 1 - me.c) * U, U)], dst_ref=Dn.at[o], send_sem=cssem.at[o], recv_sem=csem.at[o], device_id=me.core, device_id_type=MESH)
    def slot(link, d, sg, da, db, zp):
        if (da, db) == (0, 0):
            if link == "a": return zp
            if link == "b": return 4 + zp
            if d == 0 and link == "down": return 12
            return 8 + zp
        if (da, db) == (1, 0): return 13 + zp
        if d == 0 and link == "down": return 21
        return 17 + zp
    def rcopy(h, o, sl, dev):
        return pltpu.make_async_remote_copy(src_ref=P.at[o, pl.ds(h * step, step)], dst_ref=R.at[sl, pl.ds(h * step, step)], send_sem=ssem.at[h, o], recv_sem=rsem.at[h, sl], device_id=dev, device_id_type=MESH)
    def add(h, o, refs, final):
        def body(i, _):
            r = pl.ds(h * step + i * 16, 16)
            t = P[o, r, :].astype(jnp.float32)
            for f in refs: t = t + f(r).astype(jnp.float32)
            if final: out[r, :] = t
            else: P[o, r, :] = t.astype(jnp.bfloat16)
            return 0
        lax.fori_loop(0, step // 16, body, 0)
    def parent(d, sg, da, db, zp):
        z = me.z
        pd = d - 1
        def zslot(base, extra):
            if d == 1:
                return extra if sg > 0 else base + zp
            return base + zp
        toward = me.up if sg > 0 else me.down
        if (da, db) == (0, 0): return [(toward, zslot(8, 12), None)]
        if (da, db) == (1, 0): return [(me.a, zp, None)]
        if (da, db) == (0, 1): return [(me.b, 4 + zp, None)]
        if d == 0: return [(me.b, 13 + zp, None)]
        bz = byz(zp, z)
        return [(me.b, 13 + zp, jnp.logical_not(bz)), (toward, zslot(17, 21), bz)]
    for d, sg, da, db, zp, valid in evs:
        o = me.chip(zp, da, db)
        def start():
            dcopy(o).start(); load(o).start()
        when(valid, start)
    for d, sg, da, db, zp, valid in evs:
        o = me.chip(zp, da, db)
        own = (d, da, db) == (0, 0, 0)
        def go():
            load(o).wait(); dcopy(o).wait_recv()
            for h in range(sub):
                kids = children(me, d, sg, da, db, zp)
                first = True
                fixed = [lambda r: Dn[o, r, :]]
                cond_kids = []
                for link, dev, cond in kids:
                    sl = slot(link, d, sg, da, db, zp)
                    if cond is None:
                        rcopy(h, o, sl, dev).wait_recv()
                        fixed.append(lambda r, sl=sl: R[sl, r, :])
                    else: cond_kids.append((sl, dev, cond))
                for sl, dev, cond in cond_kids:
                    def g(sl=sl, dev=dev):
                        rcopy(h, o, sl, dev).wait_recv()
                        add(h, o, [lambda r: R[sl, r, :]], False)
                    pl.when(cond)(g)
                add(h, o, fixed, own)
                if not own:
                    for dev, sl, cond in parent(d, sg, da, db, zp):
                        when(cond, rcopy(h, o, sl, dev).start)
        when(valid, go)
    for d, sg, da, db, zp, valid in evs:
        o = me.chip(zp, da, db)
        def fin():
            dcopy(o).wait_send()
            if (d, da, db) != (0, 0, 0):
                for h in range(sub):
                    rcopy(h, o, 0, me.core).wait_send()
        when(valid, fin)

def reduce_scatter(part, U, sub=1, cid=2, name="scatter_grads"):
    return pl.pallas_call(functools.partial(rs_kernel, U, sub),
        out_shape=jax.ShapeDtypeStruct((U, D), jnp.float32),
        in_specs=[pl.BlockSpec(memory_space=pl.ANY)], out_specs=pl.BlockSpec(memory_space=pltpu.VMEM),
        scratch_shapes=[pltpu.VMEM((16, U, D), jnp.bfloat16), pltpu.VMEM((16, U, D), jnp.bfloat16), pltpu.VMEM((22, U, D), jnp.bfloat16),
            pltpu.SemaphoreType.DMA((sub, 16)), pltpu.SemaphoreType.DMA((sub, 22)), pltpu.SemaphoreType.DMA((16,)), pltpu.SemaphoreType.DMA((16,)), pltpu.SemaphoreType.DMA((16,))],
        compiler_params=pltpu.CompilerParams(collective_id=cid, has_side_effects=True, vmem_limit_bytes=60*2**20), name=name)(part)


UNITS = (4 * D * D + 2 * D * FF) // D
LANES = 128


def prep_kernel(k, K, U, ext, out):
    s = lax.axis_index("dp") * lax.axis_size("fsdp") + lax.axis_index("fsdp")
    off = K - k * s
    first = s * U

    def plain(i):
        for q in range(8):
            out[pl.ds(128 * i, 128), pl.ds(128 * q, 128)] = ext[pl.ds(off + 1024 * i + q, 128, stride=8), :].astype(jnp.bfloat16)

    def third(i):
        for q in range(8):
            out[pl.ds(128 * i, 128), pl.ds(128 * q, 128)] = ext[pl.ds(off + 8 * i + q, 128, stride=24), :].astype(jnp.bfloat16)

    def quarter(i):
        for j in range(4):
            for q in range(8):
                out[pl.ds(128 * i + 32 * j, 32), pl.ds(128 * q, 128)] = ext[
                    pl.ds(off + 1024 * i + 8 * j + q, 32, stride=32), :
                ].astype(jnp.bfloat16)

    for i in range(U // 128):
        place = first + 128 * i
        is_qkv = place < 3 * D
        is_up = (place >= 4 * D) & (place < 4 * D + FF)
        pl.when(is_qkv)(functools.partial(third, i))
        pl.when(is_up)(functools.partial(quarter, i))
        pl.when(jnp.logical_not(is_qkv | is_up))(functools.partial(plain, i))


def aligned_shard(flat, U):
    n = lax.axis_size("dp") * lax.axis_size("fsdp")
    lines = flat.reshape(-1, LANES)
    k = lines.shape[0] - 8 * U
    K = k * n
    tail = lax.ppermute(lines[-K:], ("dp", "fsdp"), [(i, (i + 1) % n) for i in range(n)])
    ext = jnp.concatenate([tail, lines, jnp.zeros((-lines.shape[0] % 8, LANES), jnp.float32)])
    shard = pl.pallas_call(
        functools.partial(prep_kernel, k, K, U),
        out_shape=jax.ShapeDtypeStruct((U, D), jnp.bfloat16),
        in_specs=[pl.BlockSpec(memory_space=pltpu.VMEM)],
        out_specs=pl.BlockSpec(memory_space=pltpu.VMEM),
        compiler_params=pltpu.CompilerParams(vmem_limit_bytes=32 * 2**20),
        name="align_params",
    )(ext)
    return shard, lines[-K:].reshape(K // 8, D)


def unprep_kernel(U, grad, out):
    s = lax.axis_index("dp") * lax.axis_size("fsdp") + lax.axis_index("fsdp")
    first = s * U

    def plain(i):
        for q in range(8):
            out[pl.ds(1024 * i + q, 128, stride=8), :] = grad[pl.ds(128 * i, 128), pl.ds(128 * q, 128)]

    def third(i):
        for q in range(8):
            out[pl.ds(8 * i + q, 128, stride=24), :] = grad[pl.ds(128 * i, 128), pl.ds(128 * q, 128)]

    def quarter(i):
        for j in range(4):
            for q in range(8):
                out[pl.ds(1024 * i + 8 * j + q, 32, stride=32), :] = grad[pl.ds(128 * i + 32 * j, 32), pl.ds(128 * q, 128)]

    for i in range(U // 128):
        place = first + 128 * i
        is_qkv = place < 3 * D
        is_up = (place >= 4 * D) & (place < 4 * D + FF)
        pl.when(is_qkv)(functools.partial(third, i))
        pl.when(is_up)(functools.partial(quarter, i))
        pl.when(jnp.logical_not(is_qkv | is_up))(functools.partial(plain, i))


def owned_grad(grad, table_sum, owned, U):
    n = lax.axis_size("dp") * lax.axis_size("fsdp")
    s = lax.axis_index(("dp", "fsdp"))
    k = owned // LANES - 8 * U
    K = k * n
    lines = pl.pallas_call(
        functools.partial(unprep_kernel, U),
        out_shape=jax.ShapeDtypeStruct((8 * U, LANES), jnp.float32),
        in_specs=[pl.BlockSpec(memory_space=pltpu.VMEM)],
        out_specs=pl.BlockSpec(memory_space=pltpu.VMEM),
        compiler_params=pltpu.CompilerParams(vmem_limit_bytes=32 * 2**20),
        name="flatten_grads",
    )(grad)
    follow = lax.ppermute(lines[:K], ("dp", "fsdp"), [(i, (i - 1) % n) for i in range(n)])
    table_lines = table_sum.reshape(-1, LANES)
    table_lines = jnp.pad(table_lines, ((0, K - table_lines.shape[0]), (0, 0)))
    follow = jnp.where(s == n - 1, table_lines, follow)
    ext = jnp.concatenate([lines, follow])
    return lax.dynamic_slice(ext, (k * s, 0), (owned // LANES, LANES)).reshape(-1)


def layer_mats(gathered):
    w_qkv = gathered[: 3 * D].reshape(8, 3, 128, D).transpose(0, 2, 1, 3).reshape(D, 3 * D)
    w_up = gathered[4 * D : 4 * D + FF].reshape(32, 4, 32, D).transpose(0, 2, 1, 3).reshape(D, FF)
    return w_qkv, gathered[3 * D : 4 * D], w_up, gathered[4 * D + FF :]


def layer_units(grad_wqkv, grad_wout, grad_up, grad_down):
    low = jnp.bfloat16
    return jnp.concatenate([
        grad_wqkv.astype(low).reshape(8, 128, 3, D).transpose(0, 2, 1, 3).reshape(3 * D, D),
        grad_wout.astype(low),
        grad_up.astype(low).reshape(32, 32, 4, D).transpose(0, 2, 1, 3).reshape(FF, D),
        grad_down.astype(low),
    ])


def fast_device(ar_params, nar_params, ar_moments, nar_moments, hidden_in, out_grad, phon_len, acou_len, frame_mask, section):
    n = lax.axis_size("dp") * lax.axis_size("fsdp")
    U = UNITS // n
    items_here = hidden_in.shape[0]
    position = jnp.arange(FRAMES)
    key_live = (position[None, :] < (phon_len + acou_len)[:, None]) & (
        (frame_mask == 1) | (position[None, :] == 0)
    )
    causal = position[None, :] <= position[:, None]
    prefix = position[None, None, :] < phon_len[:, None, None]
    ar_allowed = key_live[:, None, :] & (causal[None] | prefix)
    nar_allowed = jnp.broadcast_to(key_live[:, None, :], (items_here, FRAMES, FRAMES))
    ar_shard, ar_tail = aligned_shard(ar_params, U)
    nar_shard, nar_tail = aligned_shard(nar_params, U)
    is_last = lax.axis_index(("dp", "fsdp")) == n - 1
    tails = jnp.concatenate([ar_tail[:4], nar_tail[: 4 * SECTIONS]]).astype(jnp.bfloat16)
    tables = lax.psum(jnp.where(is_last, tails, 0), ("dp", "fsdp")).astype(jnp.float32)
    ar_full, nar_full = all_gather([ar_shard, nar_shard], U)
    ar_gains = tables[:4, None, :]
    nar_table = tables[4:].reshape(4, SECTIONS, D)
    onehot = (section[:, None] == jnp.arange(SECTIONS)[None, :]).astype(jnp.float32)
    nar_gains = jnp.einsum("bs,rsd->rbd", onehot, nar_table, precision=lax.Precision.HIGHEST)
    first_in = hidden_in.astype(jnp.float32)
    ar_mats, nar_mats = layer_mats(ar_full), layer_mats(nar_full)
    first_out, unused, ar_stored = trunk(first_in, ar_mats, ar_gains, ar_allowed, None)
    final, unused, nar_stored = trunk(first_out, nar_mats, nar_gains, nar_allowed, None)
    hidden_out = final.astype(jnp.bfloat16)
    grad_mid, nar_grads, nar_grad_gains = layer_back(nar_stored, nar_mats, out_grad.astype(jnp.float32))
    nar_grad_table = jnp.einsum("bs,rbd->rsd", onehot, nar_grad_gains, precision=lax.Precision.HIGHEST)
    nar_table_grad = lax.psum(nar_grad_table, ("dp", "fsdp"))
    in_grad, ar_grads, ar_grad_gains = layer_back(ar_stored, ar_mats, grad_mid)
    ar_table_grad = lax.psum(jnp.sum(ar_grad_gains, axis=1), ("dp", "fsdp"))
    nar_units = reduce_scatter(layer_units(*nar_grads), U, cid=2, name="scatter_nar")
    ar_units = reduce_scatter(layer_units(*ar_grads), U, cid=3, name="scatter_ar")
    nar_grad = owned_grad(nar_units, nar_table_grad.reshape(-1, D), nar_params.shape[0], U)
    ar_grad = owned_grad(ar_units, ar_table_grad, ar_params.shape[0], U)
    ar_step, ar_new_moments = adam_update(ar_moments, ar_grad)
    nar_step, nar_new_moments = adam_update(nar_moments, nar_grad)
    return (hidden_out, in_grad, ar_grad, nar_grad, ar_step, nar_step, ar_new_moments, nar_new_moments, nar_table_grad)


def shard_body(mesh):
    return fast_device if tuple(mesh.shape.values()) == (8, 4) else per_device


def solution(mesh):
    in_specs = (
        P(("dp", "fsdp")),
        P(("dp", "fsdp")),
        P(None, ("dp", "fsdp")),
        P(None, ("dp", "fsdp")),
        P(("dp", "fsdp"), None, None),
        P(("dp", "fsdp"), None, None),
        P(("dp", "fsdp")),
        P(("dp", "fsdp")),
        P(("dp", "fsdp"), None),
        P(("dp", "fsdp")),
    )
    out_specs = (
        P(("dp", "fsdp"), None, None),
        P(("dp", "fsdp"), None, None),
        P(("dp", "fsdp")),
        P(("dp", "fsdp")),
        P(("dp", "fsdp")),
        P(("dp", "fsdp")),
        P(None, ("dp", "fsdp")),
        P(None, ("dp", "fsdp")),
        P(),
    )
    return jax.shard_map(
        shard_body(mesh), mesh=mesh, in_specs=in_specs, out_specs=out_specs, check_vma=False
    )
```

```python
import functools

import jax
import jax.numpy as jnp
from jax import lax
from jax.experimental import pallas as pl
from jax.experimental.pallas import tpu as pltpu
from jax.sharding import PartitionSpec as P

D = 1024
FF = 4096
HEADS = 16
SECTIONS = 7
HEAD_DIM = 64
FRAMES = 384
STEP = 100


norm_eps = 1e-05
beta_one = 0.9
beta_two = 0.999
adam_eps = 1e-08


def normalize(layer_in, gain_rows, bias_rows):
    row_mean = jnp.mean(layer_in, axis=-1, keepdims=True)
    centred = layer_in - row_mean
    row_var = jnp.mean(centred * centred, axis=-1, keepdims=True)
    return centred * lax.rsqrt(row_var + norm_eps) * gain_rows[:, None, :] + bias_rows[:, None, :]


def unpack(flat_params, table_rows):
    cut_one = 3 * D * D
    cut_two = 4 * D * D
    cut_three = cut_two + D * FF
    cut_four = cut_three + FF * D
    cut_five = cut_four + 4 * table_rows * D
    matrices = (
        flat_params[:cut_one].reshape(D, 3 * D),
        flat_params[cut_one:cut_two].reshape(D, D),
        flat_params[cut_two:cut_three].reshape(D, FF),
        flat_params[cut_three:cut_four].reshape(FF, D),
    )
    return (matrices, flat_params[cut_four:cut_five].reshape(4, table_rows, D))


def collect(shard):
    tiles = shard.reshape(-1, 128)
    whole = lax.all_gather(tiles, ("dp", "fsdp"), axis=0, tiled=True)
    return whole.reshape(-1)


def spread(gradient, owned):
    total = owned * lax.axis_size("dp") * lax.axis_size("fsdp")
    padded = jnp.pad(gradient, (0, total - gradient.shape[0])).reshape(-1, 128)
    mine = lax.psum_scatter(padded, ("dp", "fsdp"), scatter_dimension=0, tiled=True)
    return mine.reshape(-1)


def trunk(layer_in, matrices, norm_gains, allowed, saved_total):
    w_qkv, w_out, w_up, w_down = matrices
    items_here = layer_in.shape[0]
    row_count = items_here * FRAMES
    score_scale = HEAD_DIM ** (-0.5)
    normed_one, first_back = jax.vjp(normalize, layer_in, norm_gains[0], norm_gains[1])
    normed_low = normed_one.astype(jnp.bfloat16).reshape(row_count, D)
    qkv_low = jnp.dot(normed_low, w_qkv, preferred_element_type=jnp.float32).astype(jnp.bfloat16)
    qkv_split = qkv_low.reshape(items_here, FRAMES, 3, HEADS, HEAD_DIM)
    queries = qkv_split[:, :, 0]
    key_rows = qkv_split[:, :, 1]
    values = qkv_split[:, :, 2]
    scores = (
        jnp.einsum("bqhd,bkhd->bhqk", queries, key_rows, preferred_element_type=jnp.float32)
        * score_scale
    )
    scores = jnp.where(allowed[:, None], scores, -jnp.inf)
    if saved_total is None:
        row_top = jnp.max(scores, axis=-1, keepdims=True)
        saved_total = row_top + jnp.log(jnp.sum(jnp.exp(scores - row_top), axis=-1, keepdims=True))
    attn_probs = jnp.exp(scores - saved_total)
    probs_low = attn_probs.astype(jnp.bfloat16)
    attended = jnp.einsum("bhqk,bkhd->bqhd", probs_low, values, preferred_element_type=jnp.float32)
    attended = attended.astype(jnp.bfloat16).reshape(row_count, D)
    middle = layer_in + jnp.dot(attended, w_out, preferred_element_type=jnp.float32).reshape(
        items_here, FRAMES, D
    )
    normed_two, second_back = jax.vjp(normalize, middle, norm_gains[2], norm_gains[3])
    second_low = normed_two.astype(jnp.bfloat16).reshape(row_count, D)
    upper = jnp.dot(second_low, w_up, preferred_element_type=jnp.float32)
    activated, gelu_back = jax.vjp(jax.nn.gelu, upper)
    act_low = activated.astype(jnp.bfloat16)
    layer_out = middle + jnp.dot(act_low, w_down, preferred_element_type=jnp.float32).reshape(
        items_here, FRAMES, D
    )
    stored = (
        first_back,
        normed_low,
        queries,
        key_rows,
        values,
        attn_probs,
        probs_low,
        attended,
        second_back,
        second_low,
        gelu_back,
        act_low,
    )
    return (layer_out, saved_total, stored)


def layer_back(stored, matrices, grad_out):
    w_qkv, w_out, w_up, w_down = matrices
    (
        first_back,
        normed_low,
        queries,
        key_rows,
        values,
        attn_probs,
        probs_low,
        attended,
        second_back,
        second_low,
        gelu_back,
        act_low,
    ) = stored
    items_here = grad_out.shape[0]
    row_count = items_here * FRAMES
    score_scale = HEAD_DIM ** (-0.5)
    grad_low = grad_out.reshape(row_count, D).astype(jnp.bfloat16)
    grad_down = jnp.einsum("rf,rd->fd", act_low, grad_low, preferred_element_type=jnp.float32)
    grad_act = jnp.einsum("rd,fd->rf", grad_low, w_down, preferred_element_type=jnp.float32)
    grad_upper = gelu_back(grad_act)[0].astype(jnp.bfloat16)
    grad_up = jnp.einsum("rd,rf->df", second_low, grad_upper, preferred_element_type=jnp.float32)
    grad_second = jnp.einsum("rf,df->rd", grad_upper, w_up, preferred_element_type=jnp.float32)
    norm_part, grad_gain_two, grad_bias_two = second_back(
        grad_second.reshape(items_here, FRAMES, D)
    )
    grad_middle = grad_out + norm_part
    branch_low = grad_middle.reshape(row_count, D).astype(jnp.bfloat16)
    grad_wout = jnp.einsum("rc,rd->cd", attended, branch_low, preferred_element_type=jnp.float32)
    grad_attended = jnp.einsum("rd,cd->rc", branch_low, w_out, preferred_element_type=jnp.float32)
    grad_attended = grad_attended.astype(jnp.bfloat16).reshape(items_here, FRAMES, HEADS, HEAD_DIM)
    grad_values = jnp.einsum(
        "bhqk,bqhd->bkhd", probs_low, grad_attended, preferred_element_type=jnp.float32
    )
    grad_probs = jnp.einsum(
        "bqhd,bkhd->bhqk", grad_attended, values, preferred_element_type=jnp.float32
    )
    row_inner = jnp.sum(attn_probs * grad_probs, axis=-1, keepdims=True)
    grad_scores = (attn_probs * (grad_probs - row_inner)).astype(jnp.bfloat16)
    grad_queries = (
        jnp.einsum("bhqk,bkhd->bqhd", grad_scores, key_rows, preferred_element_type=jnp.float32)
        * score_scale
    )
    grad_keys = (
        jnp.einsum("bhqk,bqhd->bkhd", grad_scores, queries, preferred_element_type=jnp.float32)
        * score_scale
    )
    grad_qkv = (
        jnp.stack([grad_queries, grad_keys, grad_values], axis=2)
        .astype(jnp.bfloat16)
        .reshape(row_count, 3 * D)
    )
    grad_wqkv = jnp.einsum("rc,rd->cd", normed_low, grad_qkv, preferred_element_type=jnp.float32)
    grad_first = jnp.einsum("rd,cd->rc", grad_qkv, w_qkv, preferred_element_type=jnp.float32)
    norm_in, grad_gain_one, grad_bias_one = first_back(grad_first.reshape(items_here, FRAMES, D))
    grad_in = grad_middle + norm_in
    grad_mats = (grad_wqkv, grad_wout, grad_up, grad_down)
    grad_gains = jnp.stack([grad_gain_one, grad_bias_one, grad_gain_two, grad_bias_two])
    return (grad_in, grad_mats, grad_gains)


def adam_update(moments, gradient):
    first = beta_one * moments[0] + (1.0 - beta_one) * gradient
    second = beta_two * moments[1] + (1.0 - beta_two) * gradient * gradient
    first_hat = first / (1.0 - beta_one**STEP)
    second_hat = second / (1.0 - beta_two**STEP)
    direction = first_hat / (jnp.sqrt(second_hat) + adam_eps)
    return (direction, jnp.stack([first, second]))


def per_device(
    ar_params,
    nar_params,
    ar_moments,
    nar_moments,
    hidden_in,
    out_grad,
    phon_len,
    acou_len,
    frame_mask,
    section,
):
    items_here = hidden_in.shape[0]
    position = jnp.arange(FRAMES)
    key_live = (position[None, :] < (phon_len + acou_len)[:, None]) & (
        (frame_mask == 1) | (position[None, :] == 0)
    )
    causal = position[None, :] <= position[:, None]
    prefix = position[None, None, :] < phon_len[:, None, None]
    ar_allowed = key_live[:, None, :] & (causal[None] | prefix)
    nar_allowed = jnp.broadcast_to(key_live[:, None, :], (items_here, FRAMES, FRAMES))
    ar_matrices, ar_table = unpack(collect(ar_params.astype(jnp.bfloat16)), 1)
    ar_gains = ar_table[:, 0, None, :].astype(jnp.float32)
    nar_matrices, nar_table = unpack(collect(nar_params.astype(jnp.bfloat16)), SECTIONS)
    onehot = (section[:, None] == jnp.arange(SECTIONS)[None, :]).astype(jnp.float32)
    nar_gains = jnp.einsum(
        "bs,rsd->rbd", onehot, nar_table.astype(jnp.float32), precision=lax.Precision.HIGHEST
    )
    first_in = hidden_in.astype(jnp.float32)
    first_out, unused, ar_stored = trunk(first_in, ar_matrices, ar_gains, ar_allowed, None)
    final, unused, nar_stored = trunk(first_out, nar_matrices, nar_gains, nar_allowed, None)
    hidden_out = final.astype(jnp.bfloat16)
    grad_mid, nar_grad_mats, nar_grad_gains = layer_back(nar_stored, nar_matrices, out_grad.astype(jnp.float32))
    nar_grad_table = jnp.einsum(
        "bs,rbd->rsd", onehot, nar_grad_gains, precision=lax.Precision.HIGHEST
    )
    nar_table_grad = lax.psum(nar_grad_table, ("dp", "fsdp"))
    nar_grad = spread(
        jnp.concatenate([m.reshape(-1) for m in nar_grad_mats] + [nar_grad_table.reshape(-1)]), nar_params.shape[0]
    )
    in_grad, ar_grad_mats, ar_grad_gains = layer_back(ar_stored, ar_matrices, grad_mid)
    ar_grad = spread(
        jnp.concatenate([m.reshape(-1) for m in ar_grad_mats] + [jnp.sum(ar_grad_gains, axis=1).reshape(-1)]),
        ar_params.shape[0],
    )
    ar_step, ar_new_moments = adam_update(ar_moments, ar_grad)
    nar_step, nar_new_moments = adam_update(nar_moments, nar_grad)
    return (
        hidden_out,
        in_grad,
        ar_grad,
        nar_grad,
        ar_step,
        nar_step,
        ar_new_moments,
        nar_new_moments,
        nar_table_grad,
    )


MESH = pl.DeviceIdType.MESH
NZ = 4

class Place:
    def __init__(self):
        dp = lax.axis_index("dp"); fs = lax.axis_index("fsdp")
        self.z, self.x = dp // 2, dp % 2
        self.y, self.c = fs // 2, fs % 2
        z, x, y, c = self.z, self.x, self.y, self.c
        self.a = (z * 2 + x + (1 - c) * (1 - 2 * x), (y + c * (1 - 2 * y)) * 2 + c)
        self.b = (z * 2 + x + c * (1 - 2 * x), (y + (1 - c) * (1 - 2 * y)) * 2 + c)
        self.up = (dp + 2, fs)
        self.down = (dp - 2, fs)
        self.core = (dp, y * 2 + 1 - c)
        self.shard = s = dp * 4 + fs
        self.following = ((s + 1) // 4, (s + 1) % 4)
        self.previous = ((s - 1) // 4, (s - 1) % 4)

    def chip(self, zp, da, db, c=None):
        c = self.c if c is None else c
        dx = da * (1 - c) + db * c
        dy = db * (1 - c) + da * c
        xp = self.x + dx * (1 - 2 * self.x)
        yp = self.y + dy * (1 - 2 * self.y)
        return (zp * 2 + xp) * 2 + yp

def byz(zp, z):
    return (zp == 1) | (zp == 2) | ((zp == 0) & (z == 1)) | ((zp == 3) & (z == 2))

def barrier(me):
    bar = pltpu.get_barrier_semaphore()
    def sig(dev): pl.semaphore_signal(bar, inc=1, device_id=dev, device_id_type=MESH)
    sig(me.a); sig(me.b); sig(me.core)
    pl.when(me.z < NZ - 1)(lambda: sig(me.up))
    pl.when(me.z > 0)(lambda: sig(me.down))
    pl.when(me.shard < 31)(lambda: sig(me.following))
    pl.when(me.shard > 0)(lambda: sig(me.previous))
    pl.semaphore_wait(bar, 5 + (me.z + 1) // 2 % 2 + (me.shard + 31) // 32 - me.shard // 31)

ORDER = [(0,0,0),(0,1,0),(0,0,1),(1,0,0),(0,1,1),(1,1,0),(1,0,1),(2,0,0),(1,1,1),(2,1,0),(2,0,1),(3,0,0),(2,1,1),(3,1,0),(3,0,1),(3,1,1)]

def events(me):
    out = []
    for d, da, db in ORDER:
        for sg in ((1,) if d == 0 else (1, -1)):
            zp = me.z + sg * d
            valid = None if d == 0 else ((zp < NZ) if sg > 0 else (zp >= 0))
            out.append((d, sg, da, db, zp, valid))
    return out

def children(me, d, sg, da, db, zp):
    z = me.z
    kids = []
    up_ok = (d == 0) or sg < 0
    dn_ok = (d == 0) or sg > 0
    if (da, db) == (0, 0):
        if up_ok: kids.append(("up", me.up, z < NZ - 1))
        if dn_ok: kids.append(("down", me.down, z > 0))
        kids.append(("b", me.b, None))
        kids.append(("a", me.a, None))
    elif (da, db) == (1, 0):
        kids.append(("b", me.b, None if d == 0 else jnp.logical_not(byz(zp, z))))
    elif (da, db) == (1, 1):
        if up_ok: kids.append(("up", me.up, (z < NZ - 1) & byz(zp, z + 1)))
        if dn_ok: kids.append(("down", me.down, (z > 0) & byz(zp, z - 1)))
    return kids

LINKS = {"a": 0, "b": 1, "up": 2, "down": 3, "core": 4}

def when(cond, f):
    def g(): f()
    if cond is None: g()
    else: pl.when(cond)(g)


LOW = jnp.bfloat16
F32 = jnp.float32
ROWS = FRAMES


TALL_NORM = 64


def columns(i, width):
    return pl.ds(pl.multiple_of(i * width, width), width)


def dot_nn(left, right):
    return jnp.dot(left, right, preferred_element_type=F32)


def dot_nt(left, right):
    return lax.dot_general(left, right, (((1,), (1,)), ((), ())), preferred_element_type=F32)


def dot_tn(left, right):
    return lax.dot_general(left, right, (((0,), (0,)), ((), ())), preferred_element_type=F32)


def loop(count, body, unroll=1):
    def step(i, carry):
        body(i)
        return carry

    lax.fori_loop(0, count, step, 0, unroll=unroll)


def norm_rows(src, gains, row, dst):
    def body(i):
        rows = columns(i, TALL_NORM)
        centred = src[rows, :].astype(F32)
        centred = centred - jnp.mean(centred, axis=-1, keepdims=True)
        row_var = jnp.mean(centred * centred, axis=-1, keepdims=True)
        scaled = centred * lax.rsqrt(row_var + norm_eps)
        dst[rows, :] = (scaled * gains[row : row + 1, :] + gains[row + 1 : row + 2, :]).astype(LOW)

    loop(ROWS // TALL_NORM, body)


def norm_rows_back(src, gains, row, grad, passed, dst, table, low_dst):
    table[row : row + 2, :] = jnp.zeros((2, D), F32)

    def body(i):
        rows = columns(i, TALL_NORM)
        centred = src[rows, :].astype(F32)
        centred = centred - jnp.mean(centred, axis=-1, keepdims=True)
        inverse = lax.rsqrt(jnp.mean(centred * centred, axis=-1, keepdims=True) + norm_eps)
        scaled = centred * inverse
        given = grad[rows, :]
        inner = given * gains[row : row + 1, :]
        table[row : row + 1, :] += jnp.sum(given * scaled, axis=0, keepdims=True)
        table[row + 1 : row + 2, :] += jnp.sum(given, axis=0, keepdims=True)
        along = jnp.mean(inner * scaled, axis=-1, keepdims=True)
        out = passed[rows, :].astype(F32) + inverse * (inner - jnp.mean(inner, axis=-1, keepdims=True) - scaled * along)
        dst[rows, :] = out
        if low_dst is not None:
            low_dst[rows, :] = out.astype(LOW)

    loop(ROWS // TALL_NORM, body)


def transpose_into(src, dst, base):
    def body(i):
        dst[pl.ds(pl.multiple_of(base + i * 128, 128), 128), :] = src[:, columns(i, 128)].T

    loop(D // 128, body, unroll=8)


def turn_back(src, dst):
    def body(i):
        dst[:, columns(i, 128)] = src[columns(i, 128), :].T

    loop(D // 128, body, unroll=8)


def matmul(left, right, finish, width=D):
    def body(i):
        cols = columns(i, width) if width < D else slice(None)
        finish(cols, dot_nn(left[...], right[:, cols]))

    if width < D:
        loop(D // width, body)
    else:
        body(0)


def matmul_nt(left, right, finish, width=D):
    def body(i):
        cols = columns(i, width) if width < D else slice(None)
        finish(cols, dot_nt(left[...], right[cols, :]))

    if width < D:
        loop(D // width, body)
    else:
        body(0)


TALL = ROWS
PAIRS = 2


def head_lanes(head, rows):
    lane = lax.broadcasted_iota(jnp.int32, (rows, 128), 1)
    return lane < HEAD_DIM if head == 0 else lane >= HEAD_DIM


def head_probs(queries, key_rows, bias):
    scores = dot_nt(key_rows, queries) * HEAD_DIM ** (-0.5) + bias
    exponent = jnp.exp(scores - jnp.max(scores, axis=0, keepdims=True))
    return exponent * (1.0 / jnp.sum(exponent, axis=0, keepdims=True))


def attend(qkv, bias, att_turned):
    def pair(i):
        cols = columns(i, 128)
        key_rows = qkv[1, :, cols]
        values = qkv[2, :, cols].T

        def part(r):
            rows = columns(r, TALL)
            queries = qkv[0, rows, cols]
            for head in range(2):
                own = jnp.where(head_lanes(head, TALL), queries, 0)
                probs = head_probs(own, key_rows, bias[:, rows])
                out = dot_nn(values[64 * head : 64 * head + 64, :], probs.astype(LOW))
                att_turned[pl.ds(pl.multiple_of(i * 128 + 64 * head, 64), 64), rows] = out.astype(LOW)

        loop(ROWS // TALL, part)

    loop(HEADS // 2, pair, unroll=PAIRS)


def attend_back(qkv, bias, grad_att, grad_qkv, grad_k, grad_v):
    scale = HEAD_DIM ** (-0.5)

    def pair(i):
        cols = columns(i, 128)
        key_rows, values = qkv[1, :, cols], qkv[2, :, cols]

        def part(r):
            rows = columns(r, TALL)
            queries, given = qkv[0, rows, cols], grad_att[rows, cols]
            grad_q, add_k, add_v = [], 0, 0
            for head in range(2):
                lanes_in = head_lanes(head, TALL)
                asked = jnp.where(lanes_in, queries, 0)
                probs = head_probs(asked, key_rows, bias[:, rows])
                own = jnp.where(lanes_in, given, 0)
                add_v += dot_nn(probs.astype(LOW), own)
                grad_probs = dot_nt(values, own)
                inner = jnp.sum(probs * grad_probs, axis=0, keepdims=True)
                grad_scores = (probs * (grad_probs - inner)).astype(LOW)
                add_k += dot_nn(grad_scores, asked)
                grad_q.append(dot_tn(grad_scores, key_rows))
            grad_qkv[0, rows, cols] = (jnp.where(head_lanes(0, TALL), grad_q[0], grad_q[1]) * scale).astype(LOW)
            if TALL == ROWS:
                grad_qkv[1, :, cols] = (add_k * scale).astype(LOW)
                grad_qkv[2, :, cols] = add_v.astype(LOW)
            else:
                first = r == 0
                grad_k[...] = jnp.where(first, 0.0, grad_k[...]) + add_k
                grad_v[...] = jnp.where(first, 0.0, grad_v[...]) + add_v

        loop(ROWS // TALL, part)
        if TALL != ROWS:
            grad_qkv[1, :, cols] = (grad_k[...] * scale).astype(LOW)
            grad_qkv[2, :, cols] = grad_v[...].astype(LOW)

    loop(HEADS // 2, pair, unroll=PAIRS)


def weight_piece(full, name, j):
    if name == "qkv":
        return full.at[pl.ds(0, 24)].reshape(8, 3, 128, D).at[:, j]
    if name == "out":
        return full.at[pl.ds(24, 8)]
    if name == "up":
        return full.at[pl.ds(32, 32), pl.ds(32 * j, 32)]
    return full.at[pl.ds(64 + 8 * j, 8)]


def piece_shape(name):
    return (32, 32, D) if name == "up" else (8, 128, D)


FORWARD_PIECES = [("qkv", 0), ("qkv", 1), ("qkv", 2), ("out", 0)] + [("up", j) for j in range(4)] + [("down", j) for j in range(4)]
BACKWARD_PIECES = [p for j in range(4) for p in (("down", j), ("up", j))] + [("out", 0), ("qkv", 0), ("qkv", 1), ("qkv", 2)]


class Pieces:
    def __init__(self, full, order, buf, sems, ahead=2):
        self.full, self.order, self.buf, self.sems, self.ahead = full, order, buf, sems, ahead
        self.started = self.used = 0

    def copy(self, i):
        slot = i % 3
        name, j = self.order[i]
        dst = self.buf.at[slot].reshape(*piece_shape(name))
        return pltpu.make_async_copy(weight_piece(self.full, name, j), dst, self.sems.at[slot])

    def start(self):
        while self.started < min(len(self.order), self.used + self.ahead):
            self.copy(self.started).start()
            self.started += 1

    def next(self):
        self.start()
        i = self.used
        self.copy(i).wait()
        self.used += 1
        self.start()
        return self.buf.at[i % 3]


class Saver:
    def __init__(self, sems):
        self.sems, self.copies = sems, []

    def save(self, src, dst):
        copy = pltpu.make_async_copy(src, dst, self.sems.at[len(self.copies)])
        copy.start()
        self.copies.append(copy)

    def finish(self):
        for copy in self.copies:
            copy.wait()
        self.copies = []


GELU_C = 0.7978845608028654


def forward_layer(pieces, saver, src, gains, bias, buffers, saved, out):
    normed, turned, qkv, attended, att_turned, middle, two_turned, slope, active, act_turned = buffers
    s_one, s_qkv, s_att, s_mid, s_two, s_slope, s_act = saved
    norm_rows(src, gains, 0, normed)
    transpose_into(normed, turned, 0)
    saver.save(turned, s_one)
    yield
    for j in range(3):
        weights = pieces.next()

        def put(cols, value, j=j):
            qkv[j, :, cols] = value.astype(LOW)

        matmul(normed, weights, put)
        saver.save(qkv.at[j], s_qkv.at[j])
        yield
    attend(qkv, bias, att_turned)
    saver.save(att_turned, s_att)
    turn_back(att_turned, attended)
    yield
    weights = pieces.next()

    def put_middle(cols, value):
        middle[:, cols] = src[:, cols].astype(F32) + value

    matmul(attended, weights, put_middle)
    saver.save(middle, s_mid)
    yield
    norm_rows(middle, gains, 2, normed)
    transpose_into(normed, two_turned, 0)
    saver.save(two_turned, s_two)
    yield
    for j in range(4):
        weights = pieces.next()

        def put_up(cols, value, j=j):
            inner = jnp.tanh(GELU_C * (value + 0.044715 * value * value * value))
            half = 0.5 * (1.0 + inner)
            active[j, :, cols] = (value * half).astype(LOW)
            slope[j, :, cols] = half + 0.5 * value * (1.0 - inner * inner) * (
                GELU_C * (1.0 + 3 * 0.044715 * value * value)
            )

        matmul(normed, weights, put_up)
        saver.save(slope.at[j], s_slope.at[j])
        transpose_into(active.at[j], act_turned, D * j)
        saver.save(act_turned.at[pl.ds(D * j, D)], s_act.at[pl.ds(D * j, D)])
        yield
    for j in range(4):
        weights = pieces.next()

        def put_down(cols, value, j=j):
            out[:, cols] = (middle[:, cols] if j == 0 else out[:, cols]) + value

        matmul(active.at[j], weights, put_down)
        yield


FORWARD_BUFFERS = [((ROWS, D), LOW), ((D, ROWS), LOW), ((3, ROWS, D), LOW), ((ROWS, D), LOW), ((D, ROWS), LOW), ((ROWS, D), F32),
                   ((D, ROWS), LOW), ((4, ROWS, D), F32), ((4, ROWS, D), LOW), ((FF, ROWS), LOW)]
SAVED = [((D, ROWS), LOW), ((3, ROWS, D), LOW), ((D, ROWS), LOW), ((ROWS, D), F32), ((D, ROWS), LOW), ((4, ROWS, D), F32), ((FF, ROWS), LOW)]


class Stage:
    def __init__(self, buf, full, sems):
        self.buf, self.full, self.sems = buf, full, sems
        self.count = 0
        self.copies = {}

    def slot(self):
        i = self.count % 2
        if i in self.copies:
            self.copies.pop(i).wait()
        return self.buf.at[i]

    def send(self, name, j):
        i = self.count % 2
        copy = pltpu.make_async_copy(self.buf.at[i].reshape(*piece_shape(name)), weight_piece(self.full, name, j), self.sems.at[i])
        copy.start()
        self.copies[i] = copy
        self.count += 1

    def finish(self):
        for i in list(self.copies):
            self.copies.pop(i).wait()


def backward_layer(pieces, stage, saved, loads, src, given, gains, bias, buffers, table, grad_in):
    one_t, qkv, att_t, middle, two_t, slope, act_t, given_low, grad_up, grad_two, grad_att, grad_qkv, grad_k, grad_v = buffers
    def load(ref, i, src_at=None):
        return pltpu.make_async_copy(saved[i] if src_at is None else src_at, ref, loads.at[i])
    act_copy, mid_copy, two_copy = load(act_t, 6), load(middle, 3), load(two_t, 4)
    att_copy, qkv_copy, one_copy = load(att_t, 2), load(qkv, 1), load(one_t, 0)
    def slope_copy(j):
        return pltpu.make_async_copy(saved[5].at[j], slope.at[j % 2], loads.at[7 + j % 2])
    pieces.start()
    slope_copy(0).start()
    act_copy.start()
    for copy in (two_copy, mid_copy, att_copy, qkv_copy, one_copy):
        copy.start()
    for r in range(0, ROWS, 64):
        given_low[r : r + 64, :] = given[r : r + 64, :].astype(LOW)
    yield

    def weight_grad(name, j, left, right):
        spot = stage.slot()

        spot[...] = dot_nn(left[...], right[...]).astype(LOW)
        stage.send(name, j)

    for j in range(4):
        if j < 3:
            slope_copy(j + 1).start()
        slope_copy(j).wait()
        weights = pieces.next()

        def put_act(cols, value, j=j):
            grad_up[j, :, cols] = (value * slope[j % 2, :, cols]).astype(LOW)

        matmul_nt(given_low, weights, put_act)
        yield
        weights = pieces.next()

        def put_two(cols, value, j=j):
            if j == 0:
                grad_two[:, cols] = value
            else:
                grad_two[:, cols] += value

        matmul_nt(grad_up.at[j], weights, put_two)
        yield
        if j == 0:
            act_copy.wait()
        weight_grad("down", j, act_t.at[pl.ds(D * j, D)], given_low)
        yield
    two_copy.wait()
    for j in range(4):
        weight_grad("up", j, two_t, grad_up.at[j])
        yield
    mid_copy.wait()
    norm_rows_back(middle, gains, 2, grad_two, given, grad_in, table, given_low)
    yield
    att_copy.wait()
    weight_grad("out", 0, att_t, given_low)
    yield
    weights = pieces.next()

    def put_att(cols, value):
        grad_att[:, cols] = value.astype(LOW)

    matmul_nt(given_low, weights, put_att)
    yield
    qkv_copy.wait()
    attend_back(qkv, bias, grad_att, grad_qkv, grad_k, grad_v)
    yield
    one_copy.wait()
    for j in range(3):
        weight_grad("qkv", j, one_t, grad_qkv.at[j])
        yield
    for j in range(3):
        weights = pieces.next()

        def put_one(cols, value, j=j):
            if j == 0:
                grad_two[:, cols] = value
            else:
                grad_two[:, cols] += value

        matmul_nt(grad_qkv.at[j], weights, put_one)
        yield
    norm_rows_back(src, gains, 0, grad_two, grad_in, grad_in, table, None)
    yield


BACKWARD_BUFFERS = [((D, ROWS), LOW), ((3, ROWS, D), LOW), ((D, ROWS), LOW), ((ROWS, D), F32), ((D, ROWS), LOW), ((2, ROWS, D), F32), ((FF, ROWS), LOW),
                    ((ROWS, D), LOW), ((4, ROWS, D), LOW), ((ROWS, D), F32), ((ROWS, D), LOW), ((3, ROWS, D), LOW), ((ROWS, 128), F32), ((ROWS, 128), F32)]


def vmem(shapes):
    return [pltpu.VMEM(shape, dtype) for shape, dtype in shapes]


def out_types(shapes):
    return [jax.ShapeDtypeStruct(shape, dtype) for shape, dtype in shapes]


UNITS = (4 * D * D + 2 * D * FF) // D
LANES = 128
TABLE_ROWS = 4 + 4 * SECTIONS


class Gather:
    def __init__(self, me, src, full, sends, arrivals, core_arrivals, local):
        self.me, self.src, self.full = me, src, full
        self.sends, self.arrivals, self.core_arrivals, self.local = sends, arrivals, core_arrivals, local
        self.U = src.shape[0]
        self.evs = events(me)

    def rows(self, s):
        return self.full.at[pl.ds(s * self.U, self.U)]

    def copy(self, o, s, src, link, dev):
        sem = self.core_arrivals if link == "core" else self.arrivals
        return pltpu.make_async_remote_copy(
            src_ref=src, dst_ref=self.rows(s), send_sem=self.sends.at[o, LINKS[link]], recv_sem=sem.at[o], device_id=dev, device_id_type=MESH
        )

    def own_copy(self):
        me = self.me
        return pltpu.make_async_copy(self.src, self.rows(me.shard), self.local)

    def step(self, i, finish=False):
        d, sg, da, db, zp, valid = self.evs[i]
        me = self.me
        own = i == 0
        o = me.chip(zp, da, db)
        s = o * 2 + me.c

        def go():
            src = self.src if own else self.rows(s)
            if own and not finish:
                self.own_copy().start()
            if not own and not finish:
                self.copy(o, s, src, "a", me.a).wait_recv()
            for link, dev, cond in children(me, d, sg, da, db, zp) + [("core", me.core, None)]:
                cp = self.copy(o, s, src, link, dev)
                when(cond, cp.wait_send if finish else cp.start)

        when(valid, go)

    def await_partner(self):
        me = self.me
        for o in range(16):
            s = o * 2 + 1 - me.c
            self.copy(o, s, self.rows(s), "core", me.core).wait_recv()

    def await_own(self):
        self.own_copy().wait()

    def finish(self):
        for i in range(len(self.evs)):
            self.step(i, finish=True)


def align_rows(U, k, K, me, ext, out):
    off = K - k * me.shard
    first = me.shard * U

    def put(row, start, count, stride):
        for q in range(8):
            out[pl.ds(row, count), 128 * q : 128 * q + 128] = ext[pl.ds(off + start + q, count, stride=stride), :].astype(LOW)

    def plain(i):
        put(128 * i, 1024 * i, 128, 8)

    def third(i):
        put(128 * i, 8 * i, 128, 24)

    def quarter(i):
        for j in range(4):
            put(128 * i + 32 * j, 1024 * i + 8 * j, 32, 32)

    by_kind(U, first, plain, third, quarter)


def by_kind(U, first, plain, third, quarter):
    for i in range(U // 128):
        place = first + 128 * i
        is_qkv = place < 3 * D
        is_up = (place >= 4 * D) & (place < 4 * D + FF)
        pl.when(is_qkv)(functools.partial(third, i))
        pl.when(is_up)(functools.partial(quarter, i))
        pl.when(jnp.logical_not(is_qkv | is_up))(functools.partial(plain, i))


def flatten_rows(U, me, grad, lines):
    first = me.shard * U

    def put(row, start, count, stride):
        for q in range(8):
            lines[pl.ds(start + q, count, stride=stride), :] = grad[pl.ds(row, count), 128 * q : 128 * q + 128]

    def plain(i):
        put(128 * i, 1024 * i, 128, 8)

    def third(i):
        put(128 * i, 8 * i, 128, 24)

    def quarter(i):
        for j in range(4):
            put(128 * i + 32 * j, 1024 * i + 8 * j, 32, 32)

    by_kind(U, first, plain, third, quarter)


def forward_kernel(U, *refs):
    ar_lines, nar_lines, hidden, live, select = refs[:5]
    ar_full, nar_full = refs[5:7]
    saved = refs[7:14], refs[14:21]
    first_out, hidden_out, gains = refs[21:24]
    rest = list(refs[24:])
    buffers = [rest.pop(0) for _ in FORWARD_BUFFERS]
    (wbuf, final, bias, ar_ext, nar_ext, ar_shard, nar_shard, table, ar_tail, nar_tail, ar_send_tail, nar_send_tail,
     wsem, save_sems, sends, arrivals, core_arrivals, local, ring_send, ring_recv, table_send, table_recv) = rest
    me = Place()
    layers = [(ar_lines, ar_ext, ar_shard, ar_tail, ar_send_tail), (nar_lines, nar_ext, nar_shard, nar_tail, nar_send_tail)]
    for lines, ext, shard, tail, send_tail in layers:
        K, L = tail.shape[0], lines.shape[0]
        send_tail[...] = lines[L - K :, :]
    barrier(me)

    def ring(i):
        tail, send_tail = layers[i][3:]
        return pltpu.make_async_remote_copy(
            src_ref=send_tail, dst_ref=tail, send_sem=ring_send.at[i], recv_sem=ring_recv.at[i], device_id=me.following, device_id_type=MESH
        )

    for i in range(2):
        pl.when(me.shard < 31)(ring(i).start)
    for lines, ext, shard, tail, send_tail in layers:
        K, L = tail.shape[0], lines.shape[0]
        ext[K : K + L, :] = lines[...]
    row = 0
    for i in range(2):
        tail, send_tail = layers[i][3:]
        units = tail.shape[0] // 8
        for q in range(8):
            gains_rows = send_tail[pl.ds(q, units, stride=8), :]
            final[row : row + units, 128 * q : 128 * q + 128] = gains_rows
        row += units
    gathers = [
        Gather(me, layers[i][2], (ar_full, nar_full)[i], sends.at[i], arrivals.at[i], core_arrivals.at[i], local.at[i]) for i in range(2)
    ]
    is_last = me.shard == 31

    def fill_table():
        table[...] = final[0:TABLE_ROWS, :].astype(LOW)

    pl.when(is_last)(fill_table)
    for i in range(2):
        lines, ext, shard, tail, send_tail = layers[i]
        K, L = tail.shape[0], lines.shape[0]
        pl.when(me.shard > 0)(ring(i).wait_recv)
        pl.when(me.shard < 31)(ring(i).wait_send)
        ext[0:K, :] = tail[...]
        align_rows(U, L - 8 * U, K, me, ext, shard)
        if i == 0:
            gathers[0].step(0)

    def table_copy(link, dev):
        return pltpu.make_async_remote_copy(
            src_ref=table, dst_ref=table, send_sem=table_send.at[link], recv_sem=table_recv, device_id=dev, device_id_type=MESH
        )

    pl.when(jnp.logical_not(is_last))(table_copy(0, me.down).wait_recv)
    to_x = (me.z * 2 + 1 - me.x, me.y * 2 + me.c)
    to_y = (me.z * 2 + me.x, (1 - me.y) * 2 + me.c)
    corner = (me.c == 1) & (me.y == 1)
    table_links = [
        (0, me.down, corner & (me.x == 1) & (me.z > 0)),
        (1, to_x, corner & (me.x == 1)),
        (2, to_y, corner),
        (3, me.core, me.c == 1),
    ]
    for link, dev, cond in table_links:
        pl.when(cond)(table_copy(link, dev).start)
    gains[...] = dot_nn(select[...], table[...])
    steps = len(gathers[0].evs)
    for i in range(1, steps):
        gathers[0].step(i)
        if i == steps - 6:
            gathers[1].step(0)
    gathers[0].await_own()
    gathers[0].await_partner()
    ahead = iter(range(1, steps))

    def more(count):
        for _ in range(count):
            i = next(ahead, None)
            if i is not None:
                gathers[1].step(i)

    key = lax.broadcasted_iota(jnp.int32, (ROWS, ROWS), 0)
    query = lax.broadcasted_iota(jnp.int32, (ROWS, ROWS), 1)
    is_live, is_prefix = live[:, 0:1] > 0, live[:, 1:2] > 0
    bias[...] = jnp.where(is_live & (is_prefix | (key <= query)), 0.0, -jnp.inf)
    saver = Saver(save_sems)
    pieces = Pieces(ar_full.reshape(UNITS // 128, 128, D), FORWARD_PIECES, wbuf, wsem)
    pieces.start()
    for _ in forward_layer(pieces, saver, hidden, gains.at[pl.ds(0, 8)], bias, buffers, saved[0], first_out):
        more(2)
    more(steps)
    saver.finish()
    bias[...] = jnp.where(is_live & (key >= 0), 0.0, -jnp.inf)
    gathers[1].await_own()
    gathers[1].await_partner()
    pieces = Pieces(nar_full.reshape(UNITS // 128, 128, D), FORWARD_PIECES, wbuf, wsem)
    pieces.start()
    for _ in forward_layer(pieces, saver, first_out, gains.at[pl.ds(8, 8)], bias, buffers, saved[1], final):
        pass
    hidden_out[...] = final[...].astype(LOW)
    saver.finish()
    for gather in gathers:
        gather.finish()
    for link, dev, cond in table_links:
        pl.when(cond)(table_copy(link, dev).wait_send)


ANY = pl.BlockSpec(memory_space=pl.ANY)
VM = pl.BlockSpec(memory_space=pltpu.VMEM)


def run_forward(ar_lines, nar_lines, hidden, live, select, U, K_ar, K_nar):
    low_rows = jax.ShapeDtypeStruct((ROWS, D), LOW)
    full = jax.ShapeDtypeStruct((UNITS, D), LOW)
    dma = pltpu.SemaphoreType.DMA
    return pl.pallas_call(
        functools.partial(forward_kernel, U),
        out_shape=[full, full] + out_types(SAVED) * 2 + [jax.ShapeDtypeStruct((ROWS, D), F32), low_rows, jax.ShapeDtypeStruct((16, D), F32)],
        in_specs=[VM] * 5,
        out_specs=[ANY] * 16 + [VM] * 3,
        scratch_shapes=vmem(FORWARD_BUFFERS)
        + vmem([((3, D, D), LOW), ((ROWS, D), F32), ((ROWS, ROWS), F32)])
        + vmem([((K_ar + -(-ar_lines.shape[0] // 8) * 8, LANES), F32), ((K_nar + -(-nar_lines.shape[0] // 8) * 8, LANES), F32)])
        + vmem([((U, D), LOW)] * 2 + [((TABLE_ROWS, D), LOW)] + [((K_ar, LANES), F32), ((K_nar, LANES), F32)] * 2)
        + [dma((3,)), dma((24,)), dma((2, 16, 5)), dma((2, 16)), dma((2, 16)), dma((2,)), dma((2,)), dma((2,)), dma((4,)), dma],
        compiler_params=pltpu.CompilerParams(collective_id=1, has_side_effects=True, vmem_limit_bytes=58 * 2**20),
        name="gather_and_forward",
    )(ar_lines, nar_lines, hidden, live, select)


AHEAD = 4
LATER = 6
PASSES = 2
SLOTS = 22


class Scatter:
    def __init__(self, me, part, out, bufs, sems):
        self.me, self.part, self.out = me, part, out
        self.D, self.R, self.ring = bufs
        (self.ssem, self.rsem, self.dsend, self.drecv, self.lsem, self.give, self.free) = sems
        self.U = out.shape[0]
        self.H = self.U // PASSES
        self.evs = events(me)[::-1]
        self.n = len(self.evs)
        self.total = self.n * PASSES

    def at(self, g):
        return g // self.n, self.evs[g % self.n]

    def load(self, g):
        h, (d, sg, da, db, zp, valid) = self.at(g)
        me = self.me
        s = me.chip(zp, da, db) * 2 + me.c
        i = g % (AHEAD + 1)
        return pltpu.make_async_copy(self.part.at[pl.ds(s * self.U + h * self.H, self.H)], self.ring.at[i], self.lsem.at[i])

    def partner_copy(self, g, sending):
        h, (d, sg, da, db, zp, valid) = self.at(g)
        me = self.me
        core = 1 - me.c if sending else me.c
        o = me.chip(zp, da, db, core)
        s = o * 2 + core
        return pltpu.make_async_remote_copy(
            src_ref=self.part.at[pl.ds(s * self.U + h * self.H, self.H)], dst_ref=self.D.at[o], send_sem=self.dsend.at[o],
            recv_sem=self.drecv.at[o], device_id=me.core, device_id_type=MESH,
        )

    def up_copy(self, o, slot, dev):
        return pltpu.make_async_remote_copy(
            src_ref=self.D.at[o], dst_ref=self.R.at[slot], send_sem=self.ssem.at[o], recv_sem=self.rsem.at[slot], device_id=dev, device_id_type=MESH
        )

    def start(self):
        for g in range(self.n):
            when(self.at(g)[1][5], self.partner_copy(g, True).start)
        for g in range(AHEAD):
            when(self.at(g)[1][5], self.load(g).start)

    def child_slot(self, link, d, da, db, zp):
        if (da, db) == (0, 0):
            if link == "a":
                return zp
            if link == "b":
                return 4 + zp
            return 12 if d == 0 and link == "down" else 8 + zp
        if (da, db) == (1, 0):
            return 13 + zp
        return 21 if d == 0 and link == "down" else 17 + zp

    def parents(self, d, sg, da, db, zp):
        me = self.me
        nearer = me.up if sg > 0 else me.down

        def z_slot(base, extra):
            return extra if d == 1 and sg > 0 else base + zp

        if (da, db) == (0, 0):
            return [(nearer, z_slot(8, 12), None)]
        if (da, db) == (1, 0):
            return [(me.a, zp, None)]
        if (da, db) == (0, 1):
            return [(me.b, 4 + zp, None)]
        if d == 0:
            return [(me.b, 13 + zp, None)]
        by_z = byz(zp, me.z)
        return [(me.b, 13 + zp, jnp.logical_not(by_z)), (nearer, z_slot(17, 21), by_z)]

    def add(self, o, refs, final, base):
        def body(i):
            rows = columns(i, 32)
            total = 0
            for ref in refs:
                total = total + ref[rows, :].astype(F32)
            if final:
                self.out[pl.ds(base + i * 32, 32), :] = total
            else:
                self.D[o, rows, :] = total.astype(LOW)

        loop(self.H // 32, body)

    def release(self, g):
        h, (d, sg, da, db, zp, valid) = self.at(g)
        me = self.me
        own = (d, da, db) == (0, 0, 0)

        def go():
            o = me.chip(zp, da, db)
            if not own:
                self.up_copy(o, 0, me.core).wait_send()
            if h < PASSES - 1:
                pl.semaphore_signal(self.give, inc=1, device_id=me.core, device_id_type=MESH)
                self.partner_copy(g, True).wait_send()
                pl.semaphore_wait(self.give, 1)
                self.partner_copy(g + self.n, True).start()

        when(valid, go)

    def step(self, g):
        me = self.me
        if g + AHEAD < self.total:
            when(self.at(g + AHEAD)[1][5], self.load(g + AHEAD).start)
        if g >= LATER:
            self.release(g - LATER)
        h, (d, sg, da, db, zp, valid) = self.at(g)
        own = (d, da, db) == (0, 0, 0)

        def go():
            o = me.chip(zp, da, db)
            self.load(g).wait()
            self.partner_copy(g, False).wait_recv()
            terms = [self.ring.at[g % (AHEAD + 1)], self.D.at[o]]

            def credit(dev):
                if h < PASSES - 1:
                    pl.semaphore_signal(self.free.at[o], inc=1, device_id=dev, device_id_type=MESH)

            kids = [(self.child_slot(link, d, da, db, zp), dev, cond) for link, dev, cond in children(me, d, sg, da, db, zp)]
            for slot, dev, cond in kids:
                if cond is not None:

                    def merge(slot=slot, dev=dev):
                        self.up_copy(o, slot, dev).wait_recv()
                        self.add(o, [self.D.at[o], self.R.at[slot]], False, 0)
                        credit(dev)

                    pl.when(cond)(merge)
            fixed = [(slot, dev) for slot, dev, cond in kids if cond is None]
            for slot, dev in fixed:
                self.up_copy(o, slot, dev).wait_recv()
                terms.append(self.R.at[slot])
            self.add(o, terms, own, h * self.H)
            for slot, dev in fixed:
                credit(dev)
            if not own:
                if h > 0:
                    pl.semaphore_wait(self.free.at[o], 1)
                for dev, slot, cond in self.parents(d, sg, da, db, zp):
                    when(cond, self.up_copy(o, slot, dev).start)

        when(valid, go)

    def finish(self):
        for g in range(self.total - LATER, self.total):
            self.release(g)
        for g in range(self.total - self.n, self.total):
            when(self.at(g)[1][5], self.partner_copy(g, True).wait_send)


def scatter_buffers(U):
    H = U // PASSES
    return vmem([((16, H, D), LOW), ((SLOTS, H, D), LOW), ((AHEAD + 1, H, D), LOW), ((U, D), F32)])


def scatter_sems():
    dma = pltpu.SemaphoreType.DMA
    return [dma((16,)), dma((SLOTS,)), dma((16,)), dma((16,)), dma((AHEAD + 1,)), pltpu.SemaphoreType.REGULAR, pltpu.SemaphoreType.REGULAR((16,))]


SCATTER_SEMS = 7


def hand_back(me, U, grad, lines, follow, send, recv):
    flatten_rows(U, me, grad, lines)
    K = follow.shape[0]
    copy = pltpu.make_async_remote_copy(
        src_ref=lines.at[pl.ds(0, K)], dst_ref=follow, send_sem=send, recv_sem=recv, device_id=me.previous, device_id_type=MESH
    )
    pl.when(me.shard > 0)(copy.start)
    pl.when(me.shard > 0)(copy.wait_send)
    pl.when(me.shard < 31)(copy.wait_recv)


def scatter_kernel(U, part, lines, follow, *rest):
    bufs, total = rest[:3], rest[3]
    sems = rest[4 : 4 + SCATTER_SEMS]
    send, recv = rest[4 + SCATTER_SEMS :]
    me = Place()
    barrier(me)
    scatter = Scatter(me, part, total, bufs, sems)
    scatter.start()
    for g in range(scatter.total):
        scatter.step(g)
    scatter.finish()
    hand_back(me, U, total, lines, follow, send, recv)


def run_scatter(part, U, K):
    return pl.pallas_call(
        functools.partial(scatter_kernel, U),
        out_shape=[jax.ShapeDtypeStruct((8 * U, LANES), F32), jax.ShapeDtypeStruct((K, LANES), F32)],
        in_specs=[ANY],
        out_specs=[VM, VM],
        scratch_shapes=scatter_buffers(U) + scatter_sems() + [pltpu.SemaphoreType.DMA] * 2,
        compiler_params=pltpu.CompilerParams(collective_id=3, has_side_effects=True, vmem_limit_bytes=58 * 2**20),
        name="scatter_gradient",
    )(part)


BACKWARD_SCRATCH = BACKWARD_BUFFERS + [((3, D, D), LOW), ((2, D, D), LOW)]


def backward_sems():
    dma = pltpu.SemaphoreType.DMA
    return [dma((3,)), dma((2,)), dma((9,))]


def backward_steps(full, saved, src, given, gains, bias, live, is_causal, part, table, grad_in, rest):
    buffers = rest[: len(BACKWARD_BUFFERS)]
    wbuf, stage_buf, wsem, stage_sem, loads = rest[len(BACKWARD_BUFFERS) :]
    key = lax.broadcasted_iota(jnp.int32, (ROWS, ROWS), 0)
    query = lax.broadcasted_iota(jnp.int32, (ROWS, ROWS), 1)
    shape_mask = (live[:, 1:2] > 0) | (key <= query) if is_causal else key >= 0
    pieces = Pieces(full, BACKWARD_PIECES, wbuf, wsem)
    stage = Stage(stage_buf, part, stage_sem)
    steps = backward_layer(pieces, stage, saved, loads, src, given, gains, bias, buffers, table, grad_in)
    next(steps)
    bias[...] = jnp.where((live[:, 0:1] > 0) & shape_mask, 0.0, -jnp.inf)
    yield
    yield from steps
    stage.finish()


def backward_kernel(full, *refs):
    saved, (src, given, gains, live) = refs[:7], refs[7:11]
    part, table, grad_in, bias = refs[11:15]
    for _ in backward_steps(full, saved, src, given, gains.at[pl.ds(8, 8)], bias, live, False, part, table, grad_in, refs[15:]):
        pass


BACKWARD_OUT = [((UNITS // 128, 128, D), LOW), ((4, D), F32), ((ROWS, D), F32)]


def run_backward(full, saved, src, given, gains, live):
    return pl.pallas_call(
        backward_kernel,
        out_shape=out_types(BACKWARD_OUT),
        in_specs=[ANY] * 8 + [VM] * 4,
        out_specs=[ANY, VM, VM],
        scratch_shapes=vmem([((ROWS, ROWS), F32)] + BACKWARD_SCRATCH) + backward_sems(),
        compiler_params=pltpu.CompilerParams(vmem_limit_bytes=58 * 2**20),
        name="backward_second",
    )(full, *saved, src, given, gains, live)


def scatter_backward_kernel(U, other_part, full, *refs):
    saved, (src, given, gains, live) = refs[:7], refs[7:11]
    part, table, grad_in, lines, follow, bias = refs[11:17]
    rest = refs[17:]
    n_back = len(BACKWARD_SCRATCH) + 3
    back, rest = rest[:n_back], rest[n_back:]
    bufs, total = rest[:3], rest[3]
    sems = rest[4 : 4 + SCATTER_SEMS]
    send, recv = rest[4 + SCATTER_SEMS :]
    me = Place()
    barrier(me)
    scatter = Scatter(me, other_part, total, bufs, sems)
    scatter.start()
    ahead = iter(range(scatter.total))

    def more(count):
        for _ in range(count):
            g = next(ahead, None)
            if g is not None:
                scatter.step(g)

    for _ in backward_steps(full, saved, src, given, gains.at[pl.ds(0, 8)], bias, live, True, part, table, grad_in, back):
        more(2)
    more(scatter.total)
    scatter.finish()
    hand_back(me, U, total, lines, follow, send, recv)


def run_scatter_backward(other_part, full, saved, src, given, gains, live, U, K):
    return pl.pallas_call(
        functools.partial(scatter_backward_kernel, U),
        out_shape=out_types(BACKWARD_OUT + [((8 * U, LANES), F32), ((K, LANES), F32)]),
        in_specs=[ANY] * 9 + [VM] * 4,
        out_specs=[ANY] + [VM] * 4,
        scratch_shapes=vmem([((ROWS, ROWS), F32)] + BACKWARD_SCRATCH) + backward_sems() + scatter_buffers(U) + scatter_sems() + [pltpu.SemaphoreType.DMA] * 2,
        compiler_params=pltpu.CompilerParams(collective_id=2, has_side_effects=True, vmem_limit_bytes=62 * 2**20),
        name="scatter_and_backward_first",
    )(other_part, full, *saved, src, given, gains, live)


def adam_kernel(k, lines, follow, table, moments, grad, step, new_moments, ext):
    s = lax.axis_index("dp") * lax.axis_size("fsdp") + lax.axis_index("fsdp")
    n = lax.axis_size("dp") * lax.axis_size("fsdp")
    rows, K = lines.shape[0], follow.shape[0]
    L = grad.shape[0]
    ext[0:rows, :] = lines[...]

    def end_with(ref):
        ext[rows : rows + K, :] = ref[...]

    pl.when(s == n - 1)(lambda: end_with(table))
    pl.when(s < n - 1)(lambda: end_with(follow))

    def some(start, count):
        at = pl.ds(start, count)
        g = ext[pl.ds(k * s + start, count), :]
        first = beta_one * moments[at, 0, :] + (1.0 - beta_one) * g
        second = beta_two * moments[at, 1, :] + (1.0 - beta_two) * g * g
        grad[at, :] = g
        step[at, :] = (first / (1.0 - beta_one**STEP)) / (jnp.sqrt(second / (1.0 - beta_two**STEP)) + adam_eps)
        new_moments[at, 0, :] = first
        new_moments[at, 1, :] = second

    loop(L // 64, lambda i: some(pl.multiple_of(i * 64, 64), 64))
    if L % 64:
        some(L // 64 * 64, L % 64)


def run_adam(lines, follow, table, moments, name):
    L = moments.shape[1] // LANES
    K = follow.shape[0]
    paired = moments.reshape(2, L, LANES).transpose(1, 0, 2)
    flat = jax.ShapeDtypeStruct((L, LANES), F32)
    table = jnp.pad(table.reshape(-1, LANES), ((0, K - table.size // LANES), (0, 0)))
    grad, step, new = pl.pallas_call(
        functools.partial(adam_kernel, L - lines.shape[0]),
        out_shape=[flat, flat, jax.ShapeDtypeStruct((L, 2, LANES), F32)],
        in_specs=[VM] * 4,
        out_specs=[VM] * 3,
        scratch_shapes=vmem([((lines.shape[0] + K, LANES), F32)]),
        compiler_params=pltpu.CompilerParams(vmem_limit_bytes=40 * 2**20),
        name=name,
    )(lines, follow, table, paired)
    return grad.reshape(-1), step.reshape(-1), new.transpose(1, 0, 2).reshape(2, L * LANES)


def fast_device(ar_params, nar_params, ar_moments, nar_moments, hidden_in, out_grad, phon_len, acou_len, frame_mask, section):
    n = lax.axis_size("dp") * lax.axis_size("fsdp")
    U = UNITS // n
    ar_lines, nar_lines = ar_params.reshape(-1, LANES), nar_params.reshape(-1, LANES)
    K_ar, K_nar = (ar_lines.shape[0] - 8 * U) * n, (nar_lines.shape[0] - 8 * U) * n
    position = jnp.arange(FRAMES)
    key_live = (position < phon_len + acou_len) & ((frame_mask[0] == 1) | (position == 0))
    live = jnp.stack([key_live, position < phon_len], axis=1).astype(F32)
    row = jnp.arange(16)[:, None]
    entry = jnp.where(row < 4, row, 4 + SECTIONS * (row - 8) + section[0])
    select = ((jnp.arange(TABLE_ROWS)[None, :] == entry) & (row % 8 < 4)).astype(LOW)
    outs = run_forward(ar_lines, nar_lines, hidden_in[0], live, select, U, K_ar, K_nar)
    ar_full, nar_full = (full.reshape(UNITS // 128, 128, D) for full in outs[:2])
    ar_saved, nar_saved = outs[2:9], outs[9:16]
    first_out, hidden_out, gains = outs[16:]
    nar_part, nar_table, grad_mid = run_backward(nar_full, nar_saved, first_out, out_grad[0], gains, live)
    onehot = (section[:, None] == jnp.arange(SECTIONS)[None, :]).astype(F32)
    nar_table_grad = lax.psum(onehot[0][None, :, None] * nar_table[:, None, :], ("dp", "fsdp"))
    ar_part, ar_table, in_grad, nar_rows, nar_follow = run_scatter_backward(
        nar_part.reshape(UNITS, D), ar_full, ar_saved, hidden_in[0], grad_mid, gains, live, U, K_nar
    )
    ar_table_grad = lax.psum(ar_table, ("dp", "fsdp"))
    ar_rows, ar_follow = run_scatter(ar_part.reshape(UNITS, D), U, K_ar)
    nar_grad, nar_step, nar_new_moments = run_adam(nar_rows, nar_follow, nar_table_grad, nar_moments, "adam_second")
    ar_grad, ar_step, ar_new_moments = run_adam(ar_rows, ar_follow, ar_table_grad, ar_moments, "adam_first")
    return (hidden_out[None], in_grad[None], ar_grad, nar_grad, ar_step, nar_step, ar_new_moments, nar_new_moments, nar_table_grad)


def shard_body(mesh):
    return fast_device if tuple(mesh.shape.values()) == (8, 4) else per_device


def solution(mesh):
    in_specs = (
        P(("dp", "fsdp")),
        P(("dp", "fsdp")),
        P(None, ("dp", "fsdp")),
        P(None, ("dp", "fsdp")),
        P(("dp", "fsdp"), None, None),
        P(("dp", "fsdp"), None, None),
        P(("dp", "fsdp")),
        P(("dp", "fsdp")),
        P(("dp", "fsdp"), None),
        P(("dp", "fsdp")),
    )
    out_specs = (
        P(("dp", "fsdp"), None, None),
        P(("dp", "fsdp"), None, None),
        P(("dp", "fsdp")),
        P(("dp", "fsdp")),
        P(("dp", "fsdp")),
        P(("dp", "fsdp")),
        P(None, ("dp", "fsdp")),
        P(None, ("dp", "fsdp")),
        P(),
    )
    return jax.shard_map(
        shard_body(mesh), mesh=mesh, in_specs=in_specs, out_specs=out_specs, check_vma=False
    )
```
